32 devices in a mesh: au: 4 (over y, x), vert: 4 (over z), af: 2 (over core).
Axes of the slice: x: 2, y: 2, z: 4, core: 2. Of those that a mesh axis runs over, the one named last changes fastest.
Arguments:
- visib: float32 [2, 256, 1024], P('af', ('au', 'vert')), may hold values from -6 to 6
- coords: float32 [2, 256, 1024], P('af', ('au', 'vert')), may hold values from -16 to 16
- owner: int32 [2, 256], P('af', ('au', 'vert')), may hold values from 0 to 15, as said below
- offsets: int32 [2, 256, 2], P('af', ('au', 'vert')), may hold values from 0 to 448
- stations: int32 [2, 256, 2], P('af', ('au', 'vert')), may hold values from 0 to 511, as said below
- live: int32 [2, 16], P('af', ('au', 'vert')), may hold values from 16 to 16, as said below
- beams: bfloat16 [2, 512, 8192], P('af', ('au', 'vert')), may hold values from -4.1875 to 4.1875
- taper: float32 [2048, 2048], P('au', 'vert'), may hold values from 0.5 to 2
Outputs:
- predicted: float32 [2, 256, 1024], P('af', ('au', 'vert'))
- model_grid: float32 [2, 2048, 2048], P(None, 'au', 'vert')
The draws below stay inside these ranges and needn't reach their ends.
Inputs may be any that keep to these rules, and one draw needn't show every extreme that they name: A tile id is tile row times the number of tile columns plus tile column. The owner of a live block is its holder's tile or one of the eight tiles around it inside the grid; the owner of a dead block is its holder's tile. Among the live blocks of one holder, at most 2 name any one other tile, and in every channel group one tile receives exactly 2 blocks from each of its eight neighbours. The two stations of a block differ. Counting both stations of all 16 blocks of one holder, at most 4 of these entries lie on the stations s of any one value of s // 32, and some value takes exactly 4 on every holder. In every channel group some holder has all 16 blocks live.
All inputs are finite; a program needn't handle non-finite values.
Results may differ from the reference program's by a relative error of at most 0.0004.
Values may be sent and summed in bfloat16 or wider, within the bound.
A program may use at most 64 MiB of HBM per device.

```python
import math
import jax
import jax.numpy as jnp
from jax import lax

S = 64
STATIONS = 512
ROWS = 512
CAP = 2
NB = 16
TS = 512
NGRP = 2
BLOCKS = 256
NU = 2048
NV = 2048
N_AU = 4
N_VERT = 4


def block_plan(key):
    tile_total = N_AU * N_VERT
    base_key = jax.random.fold_in(key, 11)
    key_live, key_full, key_row, key_col, key_count, key_order = jax.random.split(base_key, 6)
    live_count = jax.random.randint(key_live, (NGRP, tile_total), 8 * CAP, NB + 1)
    fullest = jax.random.randint(key_full, (NGRP, 1), 0, tile_total)
    tile_ids = jnp.arange(tile_total, dtype=jnp.int32)
    live_count = jnp.where(tile_ids[None, :] == fullest, NB, live_count)
    busy_row = jax.random.randint(key_row, (NGRP, 1, 1), 1, N_AU - 1)
    busy_col = jax.random.randint(key_col, (NGRP, 1, 1), 1, N_VERT - 1)
    route_ids = jnp.arange(9, dtype=jnp.int32)
    step_row = route_ids // 3 - 1
    step_col = route_ids % 3 - 1
    dest_row = (tile_ids // N_VERT)[None, :, None] + step_row[None, None, :]
    dest_col = (tile_ids % N_VERT)[None, :, None] + step_col[None, None, :]
    inside = (dest_row >= 0) & (dest_row < N_AU) & (dest_col >= 0) & (dest_col < N_VERT) & (route_ids != 4)[None, None, :]
    counts = jax.random.randint(key_count, (NGRP, tile_total, 9), 0, CAP + 1)
    is_busy = (dest_row == busy_row) & (dest_col == busy_col)
    counts = jnp.where(is_busy, CAP, counts)
    counts = jnp.where(inside, counts, 0)
    ends_at = jnp.cumsum(counts, axis=2)
    sequence = jnp.arange(NB, dtype=jnp.int32)
    seq_route = jnp.sum((ends_at[:, :, None, :] <= sequence[None, None, :, None]).astype(jnp.int32), axis=3)
    seq_route = jnp.where(seq_route >= 9, 4, seq_route)
    scores = jax.random.randint(key_order, (NGRP, tile_total, NB), 0, 1 << 20)
    scores = jnp.where(sequence[None, None, :] < live_count[:, :, None], scores, (1 << 20) + sequence[None, None, :])
    scores = scores * NB + sequence[None, None, :]
    order_of = jnp.argsort(scores, axis=2, stable=True)
    inverse = jnp.argsort(order_of, axis=2, stable=True)
    block_route = jnp.take_along_axis(seq_route, inverse, axis=2)
    own_row = (tile_ids // N_VERT)[None, :, None] + block_route // 3 - 1
    own_col = (tile_ids % N_VERT)[None, :, None] + block_route % 3 - 1
    owner_ids = own_row * N_VERT + own_col
    return (live_count.astype(jnp.int32), owner_ids.reshape(NGRP, tile_total * NB).astype(jnp.int32))


def draw_live(key, part):
    return block_plan(key)[0]


def draw_owner(key, part):
    return block_plan(key)[1]


def draw_stations(key, part):
    tile_total = N_AU * N_VERT
    ask_total = 2 * NB
    per_dev = STATIONS // tile_total
    ask_cap = ask_total // tile_total + 2
    full_most = ask_total // ask_cap
    base_key = jax.random.fold_in(key, 23)
    key_full, key_owner, key_shuffle, key_local = jax.random.split(base_key, 4)
    full_groups = jax.random.randint(key_full, (NGRP, tile_total, 1), 1, full_most + 1)
    ask_index = jnp.arange(ask_total, dtype=jnp.int32)[None, None, :]
    slot_group = jnp.where(ask_index < full_groups * ask_cap, ask_index // ask_cap, full_groups + (ask_index - full_groups * ask_cap) % (tile_total - full_groups))
    owner_scores = jax.random.randint(key_owner, (NGRP, tile_total, tile_total), 0, 1 << 20) * tile_total + jnp.arange(tile_total, dtype=jnp.int32)
    owner_perm = jnp.argsort(owner_scores, axis=2, stable=True).astype(jnp.int32)
    keeper = jnp.take_along_axis(owner_perm, slot_group, axis=2)
    ask_scores = jax.random.randint(key_shuffle, (NGRP, tile_total, ask_total), 0, 1 << 20) * ask_total + jnp.arange(ask_total, dtype=jnp.int32)
    shuffle = jnp.argsort(ask_scores, axis=2, stable=True)
    keeper = jnp.take_along_axis(keeper, shuffle, axis=2).reshape(NGRP, tile_total, NB, 2)
    local_id = jax.random.randint(key_local, (NGRP, tile_total, ask_total), 0, per_dev).reshape(NGRP, tile_total, NB, 2)
    first = keeper[..., 0] * per_dev + local_id[..., 0]
    clash = (keeper[..., 0] == keeper[..., 1]) & (local_id[..., 0] == local_id[..., 1])
    second_local = jnp.where(clash, (local_id[..., 1] + 1) % per_dev, local_id[..., 1])
    second = keeper[..., 1] * per_dev + second_local
    return jnp.stack([first, second], axis=-1).reshape(NGRP, tile_total * NB, 2).astype(jnp.int32)


def plant(values, rng, low, high):
    longest = values.shape.index(max(values.shape))
    spots = []
    for shift in (0, 1):
        where = [jax.random.randint(jax.random.fold_in(rng, axis), (), 0, length) for axis, length in enumerate(values.shape)]
        where[longest] = (where[longest] + shift) % values.shape[longest]
        spots.append(tuple(where))
    return values.at[spots[0]].set(low).at[spots[1]].set(high)


def level_of(key, shape, shards, smallest, largest):
    factor_of, own = 1.0, jax.random.fold_in(key, 6)
    for dim, blocks in shards:
        draws = jnp.exp(jax.random.uniform(jax.random.fold_in(own, dim), (blocks,), jnp.float32, smallest / len(shards), largest / len(shards)))
        factor_of = factor_of * jnp.repeat(draws, shape[dim] // blocks).reshape([-1 if axis == dim else 1 for axis in range(len(shape))])
    return factor_of


def gaussian(rng, dims, width, most, cuts=(), kind=jnp.bfloat16):
    values = jax.random.normal(rng, dims, jnp.float32) * width
    if len(cuts) > 0:
        values = level_of(rng, dims, cuts, -0.22, 0.18) * values
    return jnp.clip(values, min=-most, max=most).astype(kind)


def setup_inputs(seed: int = 0) -> dict:
    arg_keys = jax.random.split(jax.random.key(seed), 9)
    visib = gaussian(arg_keys[0], (NGRP, BLOCKS, 2 * ROWS), 1.0, 6.0, ((0, 2), (1, 16)), jnp.float32)
    coords = jnp.clip(jax.random.uniform(arg_keys[1], (NGRP, BLOCKS, 2 * ROWS), jnp.float32, -16.0, 16.0) * level_of(arg_keys[1], (NGRP, BLOCKS, 2 * ROWS), ((0, 2), (1, 16)), -0.4, 0.0), -16.0, 16.0)
    owner = draw_owner(jax.random.fold_in(arg_keys[8], 71), 0)
    offsets = plant(jax.random.randint(arg_keys[3], (NGRP, BLOCKS, 2), 0, TS - S + 1), jax.random.fold_in(arg_keys[3], 1), 0, TS - S).astype(jnp.int32)
    stations = draw_stations(jax.random.fold_in(arg_keys[8], 71), 0)
    live = draw_live(jax.random.fold_in(arg_keys[8], 71), 0)
    beams = gaussian(arg_keys[6], (NGRP, STATIONS, 2 * S * S), 0.7, 4.1875, ((0, 2), (1, 16)))
    taper = jnp.clip(jnp.exp(math.log(2.0) - 1.3862944 * jax.random.uniform(arg_keys[7], (NU, NV), jnp.float32) ** level_of(arg_keys[7], (NU, NV), ((0, 4), (1, 4)), -0.2, 0.2)), 0.5, 2.0)
    return dict(visib=visib, coords=coords, owner=owner, offsets=offsets, stations=stations, live=live, beams=beams, taper=taper)


highest = lax.Precision.HIGHEST

def tables(side_len):
    positions = jnp.arange(side_len, dtype=jnp.int32)
    wrapped = positions[:, None] * positions[None, :] % side_len
    angles = wrapped.astype(jnp.float32) * (2.0 * math.pi / side_len)
    scaling = 1.0 / math.sqrt(side_len)
    return (jnp.cos(angles) * scaling, -jnp.sin(angles) * scaling)

def rotate(values):
    half_width = values.shape[-1] // 2
    return jnp.concatenate([-values[..., half_width:], values[..., :half_width]], axis=-1)

def complex_mul(values, factor):
    half_width = values.shape[-1] // 2
    x_real, x_imag = (values[..., :half_width], values[..., half_width:])
    a_real, a_imag = (factor[..., :half_width], factor[..., half_width:])
    return jnp.concatenate([x_real * a_real - x_imag * a_imag, x_real * a_imag + x_imag * a_real], axis=-1)

def conj_mul(values, factor):
    half_width = values.shape[-1] // 2
    x_real, x_imag = (values[..., :half_width], values[..., half_width:])
    a_real, a_imag = (factor[..., :half_width], factor[..., half_width:])
    return jnp.concatenate([x_real * a_real + x_imag * a_imag, x_imag * a_real - x_real * a_imag], axis=-1)

def phases(coords_in, side_len):
    centre = jnp.arange(side_len, dtype=jnp.float32) - side_len / 2
    angles = coords_in[..., None] * centre * (2.0 * math.pi / side_len)
    return (jnp.cos(angles), jnp.sin(angles))

def grid_blocks(visib_rows, coord_rows, beam_terms):
    row_count = visib_rows.shape[-1] // 2
    side_len = beam_terms.shape[-2]
    cos_u, sin_u = phases(coord_rows[..., :row_count], side_len)
    cos_v, sin_v = phases(coord_rows[..., row_count:], side_len)
    vis_real = visib_rows[..., :row_count, None]
    vis_imag = visib_rows[..., row_count:, None]
    weighted = jnp.concatenate([vis_real * cos_v - vis_imag * sin_v, vis_real * sin_v + vis_imag * cos_v], axis=-1)
    first = jnp.einsum('krl,krc->klc', cos_u, weighted, precision=highest)
    second = jnp.einsum('krl,krc->klc', sin_u, weighted, precision=highest)
    image_part = (first + rotate(second)) * (1.0 / math.sqrt(row_count))
    image_part = complex_mul(image_part, beam_terms)
    table_real, table_imag = tables(side_len)
    left_side = jnp.einsum('al,klc->kac', table_real, image_part, precision=highest)
    left_side = left_side + rotate(jnp.einsum('al,klc->kac', table_imag, image_part, precision=highest))
    right_side = jnp.concatenate([jnp.concatenate([table_real, table_imag], 1), jnp.concatenate([-table_imag, table_real], 1)], 0)
    return jnp.einsum('kac,cd->kad', left_side, right_side, precision=highest)

def degrid_blocks(windows, coord_rows, beam_terms):
    side_len = windows.shape[-2]
    row_count = coord_rows.shape[-1] // 2
    table_real, table_imag = tables(side_len)
    left_side = jnp.einsum('al,klc->kac', table_real, windows, precision=highest)
    left_side = left_side - rotate(jnp.einsum('al,klc->kac', table_imag, windows, precision=highest))
    right_side = jnp.concatenate([jnp.concatenate([table_real, -table_imag], 1), jnp.concatenate([table_imag, table_real], 1)], 0)
    image_part = jnp.einsum('kac,cd->kad', left_side, right_side, precision=highest)
    image_part = conj_mul(image_part, beam_terms)
    cos_u, sin_u = phases(coord_rows[..., :row_count], side_len)
    cos_v, sin_v = phases(coord_rows[..., row_count:], side_len)
    first = jnp.einsum('krl,klc->krc', cos_u, image_part, precision=highest)
    second = jnp.einsum('krl,klc->krc', sin_u, image_part, precision=highest)
    along_rows = first - rotate(second)
    a_real = along_rows[..., :side_len]
    a_imag = along_rows[..., side_len:]
    real_part = lax.optimization_barrier(jnp.sum(a_real * cos_v + a_imag * sin_v, axis=-1))
    imag_part = lax.optimization_barrier(jnp.sum(a_imag * cos_v - a_real * sin_v, axis=-1))
    return jnp.concatenate([real_part, imag_part], axis=-1) * (1.0 / side_len)

def group_terms(beam_rows, pair_ids):
    block_total = pair_ids.shape[0]
    first = jnp.take(beam_rows, pair_ids[:, 0], axis=0).astype(jnp.float32).reshape(block_total, S, 2 * S)
    second = jnp.take(beam_rows, pair_ids[:, 1], axis=0).astype(jnp.float32).reshape(block_total, S, 2 * S)
    return conj_mul(first, second)

def reference(visib, coords, owner, offsets, stations, live, beams, taper):
    block_ids = jnp.arange(BLOCKS, dtype=jnp.int32)
    zero_index = jnp.zeros((), jnp.int32)

    def positions_of(group_id):
        tile_ids = owner[group_id].astype(jnp.int32)
        shifts_in = offsets[group_id].astype(jnp.int32)
        row_start = (tile_ids // N_VERT * TS + shifts_in[:, 0]).astype(jnp.int32)
        col_start = (tile_ids % N_VERT * TS + shifts_in[:, 1]).astype(jnp.int32)
        counts_in = live[group_id].astype(jnp.int32)
        is_alive = (block_ids % NB < counts_in[block_ids // NB]).astype(jnp.float32)
        return (row_start, col_start, is_alive)

    def add_group(group_id, summed_grid):
        row_start, col_start, is_alive = positions_of(group_id)
        beam_terms = group_terms(beams[group_id], stations[group_id])
        subgrids = grid_blocks(visib[group_id], coords[group_id], beam_terms) * is_alive[:, None, None]

        def add_one(block_at, partial_value):
            subgrid = subgrids[block_at].reshape(S, 2, S).transpose(1, 0, 2)
            corner = (zero_index, row_start[block_at], col_start[block_at])
            window = lax.dynamic_slice(partial_value, corner, (2, S, S))
            return lax.dynamic_update_slice(partial_value, window + subgrid, corner)
        return lax.fori_loop(0, BLOCKS, add_one, summed_grid)
    summed_grid = lax.fori_loop(0, NGRP, add_group, jnp.zeros((2, NU, NV), jnp.float32))
    model_grid = summed_grid * taper[None]

    def predict(group_id):
        row_start, col_start, is_alive = positions_of(group_id)
        beam_terms = group_terms(beams[group_id], stations[group_id])

        def cut_window(row_at, col_at):
            return lax.dynamic_slice(model_grid, (zero_index, row_at, col_at), (2, S, S))
        windows = jax.vmap(cut_window)(row_start, col_start)
        windows = jnp.transpose(windows, (0, 2, 1, 3)).reshape(BLOCKS, S, 2 * S)
        return degrid_blocks(windows, coords[group_id], beam_terms) * is_alive[:, None]
    predicted = lax.map(predict, jnp.arange(NGRP, dtype=jnp.int32))
    return (predicted, model_grid)
```

```python
import math

import jax
import jax.numpy as jnp
import numpy as np
from jax import lax
from jax.experimental import pallas as pl
from jax.experimental.pallas import tpu as pltpu
from jax.sharding import PartitionSpec as P

S = 64
CAP = 2
NB = 16
TS = 512
BF = jnp.bfloat16
F32 = jnp.float32
MESH = pl.DeviceIdType.MESH
ROUTES = tuple((r, c) for r in (-1, 0, 1) for c in (-1, 0, 1) if (r, c) != (0, 0))
NR = len(ROUTES)
NSLOT = NR * CAP + NB
VMEM_LIMIT = 56 * 1024 * 1024


def fit(fn, count):
    k = np.arange(400)
    z = 0.125 * (1.0 + np.cos(np.pi * (k + 0.5) / 400))
    cheb = np.polynomial.chebyshev.Chebyshev.fit(z, fn(np.sqrt(z)), count - 1, domain=[0, 0.25])
    return [float(v) for v in cheb.convert(kind=np.polynomial.Polynomial).coef]


COS = fit(lambda t: np.cos(2 * np.pi * t), 8)
SIN = fit(lambda t: np.sin(2 * np.pi * t) / t, 8)


def dft_tables():
    pos = np.arange(S)
    ang = (pos[:, None] * pos[None, :] % S) * (2.0 * np.pi / S)
    return np.cos(ang) / math.sqrt(S), -np.sin(ang) / math.sqrt(S)


def split_np(x):
    x = x.astype(np.float32)
    hi = x.astype(BF).astype(np.float32)
    return hi, (x - hi).astype(BF).astype(np.float32)


def constants():
    fr, fi = dft_tables()
    hi, lo = split_np(np.concatenate([fr, fi], 0))
    left = np.concatenate([hi, hi, lo, lo], 1)
    out = [left]
    for sign in (1, -1):
        right = np.concatenate(
            [np.concatenate([fr, sign * fi], 1), np.concatenate([-sign * fi, fr], 1)], 0
        )
        hi, lo = split_np(right)
        out.append(np.concatenate([np.concatenate([hi, hi], 0), np.concatenate([lo, lo], 0)], 1))
    return [v.astype(BF) for v in out]


def split(x):
    hi = x.astype(BF)
    return hi, (x - hi.astype(F32)).astype(BF)


def horner(coefs, z):
    acc = jnp.full(z.shape, coefs[-1], F32)
    for c in coefs[-2::-1]:
        acc = acc * z + c
    return acc


def cos_sin(turns):
    t = turns - jnp.round(turns)
    z = t * t
    return horner(COS, z), horner(SIN, z) * t


def phases(u):
    j = lax.broadcasted_iota(jnp.int32, (8, u.shape[1]), 0).astype(F32)
    c1, s1 = cos_sin(u * (j * (1.0 / 64)))
    c2, s2 = cos_sin(u * (j * 0.125 - 0.5))
    cs, ss = [], []
    for k in range(8):
        ck, sk = c2[k : k + 1], s2[k : k + 1]
        cs.append(ck * c1 - sk * s1)
        ss.append(sk * c1 + ck * s1)
    return jnp.concatenate(cs, 0), jnp.concatenate(ss, 0)


def low_half(shape):
    return lax.broadcasted_iota(jnp.int32, shape, 1) < S


def rotate(x):
    y = pltpu.roll(x, S, 1)
    return jnp.where(low_half(x.shape), -y, y)


def times(x, a, conj):
    low = low_half(x.shape)
    ra = pltpu.roll(a, S, 1)
    rr = jnp.where(low, a, ra)
    ii = jnp.where(low, ra, a)
    y = pltpu.roll(x, S, 1) * ii
    sgn = low if conj else jnp.logical_not(low)
    return x * rr + jnp.where(sgn, y, -y)


def dft2(x, left, right, conj):
    hi, lo = split(x)
    m = jnp.dot(left, jnp.concatenate([hi, lo, hi, lo], 0), preferred_element_type=F32)
    turned = rotate(m[S:])
    y = m[:S] - turned if conj else m[:S] + turned
    hi, lo = split(y)
    m = jnp.dot(jnp.concatenate([hi, lo], 1), right, preferred_element_type=F32)
    return m[:, : 2 * S] + m[:, 2 * S :]


def image_kernel(vis_ref, coord_ref, out_ref):
    rows = vis_ref.shape[1] // 2

    def step(b, _):
        at = pl.ds(b, 1)
        cu, su = phases(coord_ref[at, :rows])
        cv, sv = phases(coord_ref[at, rows:])
        vr, vi = vis_ref[at, :rows], vis_ref[at, rows:]
        ahi, alo = split(jnp.concatenate([cu, su], 0))
        bhi, blo = split(jnp.concatenate([vr * cv - vi * sv, vr * sv + vi * cv], 0))
        m = lax.dot_general(
            jnp.concatenate([ahi, alo], 0),
            jnp.concatenate([bhi, blo], 0),
            (((1,), (1,)), ((), ())),
            preferred_element_type=F32,
        )
        m = m[: 2 * S] + m[2 * S :]
        m = m[:, : 2 * S] + m[:, 2 * S :]
        out_ref[b] = (m[:S] + rotate(m[S:])) * (1.0 / math.sqrt(rows))
        return 0

    lax.fori_loop(0, NB, step, 0)


def subgrid_kernel(n_vert, per_dev, cap, me_ref, info_ref, image_ref, beam_ref, left_ref, right_ref,
                   out_ref, aterm_ref, where_ref, count_ref, heads_ref):
    me = me_ref[0]
    n = info_ref.shape[0]
    row, col = me // n_vert, me % n_vert

    def zero(i, _):
        count_ref[i] = 0
        return 0

    lax.fori_loop(0, n, zero, 0)
    for i in range(9):
        heads_ref[i] = 0
    live = info_ref[me, 5 * NB]

    def find(station):
        keeper = station // per_dev
        order = count_ref[keeper]
        count_ref[keeper] = order + 1
        return lax.rem(me - keeper + n, n) * cap + order

    def step(b, _):
        first = find(info_ref[me, 3 * NB + b])
        second = find(info_ref[me, 4 * NB + b])
        owner = info_ref[me, b]
        head = (owner // n_vert - row + 1) * 3 + (owner % n_vert - col + 1)
        head = jnp.where(b < live, head, 4)
        order = heads_ref[head]
        heads_ref[head] = order + 1
        slot = jnp.where(head == 4, NR * CAP + b, jnp.where(head < 4, head, head - 1) * CAP + order)
        where_ref[b] = slot
        p = beam_ref[first].astype(F32)
        q = beam_ref[second].astype(F32)
        aterm = times(p, q, True)
        aterm_ref[b] = aterm
        out_ref[slot] = dft2(times(image_ref[b], aterm, False), left_ref[...], right_ref[...], False)
        return 0

    lax.fori_loop(0, NB, step, 0)


def incoming(n_vert, n_au, me, info_ref, visit):
    row, col = me // n_vert, me % n_vert
    for route, (dr, dc) in enumerate(ROUTES):
        sr, sc = row - dr, col - dc
        inside = (sr >= 0) & (sr < n_au) & (sc >= 0) & (sc < n_vert)

        @pl.when(inside)
        def _(route=route, src=sr * n_vert + sc):
            live = info_ref[src, 5 * NB]

            def look(b, count):
                hit = info_ref[src, b] == me

                @pl.when(hit)
                def _():
                    visit(route * CAP + count, info_ref[src, NB + b], info_ref[src, 2 * NB + b])

                return count + hit.astype(jnp.int32)

            lax.fori_loop(0, live, look, jnp.int32(0))

    def own(b, _):
        @pl.when(info_ref[me, b] == me)
        def _():
            visit(NR * CAP + b, info_ref[me, NB + b], info_ref[me, 2 * NB + b])

        return 0

    lax.fori_loop(0, info_ref[me, 5 * NB], own, 0)


def tile_kernel(n_vert, n_au, me_ref, info_ref, got_ref, mine_ref, out_ref, pad_ref):
    pad_ref[...] = jnp.zeros_like(pad_ref)
    low = low_half((S, 2 * S))
    blank = jnp.zeros((S, 2 * S), F32)
    blank_rows = jnp.zeros((8, 256), F32)

    def visit(slot, row_at, col_at):
        top = pl.multiple_of(row_at // 8 * 8, 8)
        start = pl.multiple_of(col_at // 128 * 128, 128)
        shift = col_at % 128

        def put(x):
            for plane in range(2):
                part = x if plane == 0 else pltpu.roll(x, S, 1)
                wide = jnp.concatenate([jnp.where(low, part, 0.0), blank], 1)
                wide = jnp.concatenate([pltpu.roll(wide, shift, 1), blank_rows], 0)
                at = (plane, pl.ds(top, S + 8), pl.ds(start, 256))
                pad_ref[at] += pltpu.roll(wide, row_at % 8, 0)

        @pl.when(slot < NR * CAP)
        def _():
            put(got_ref[jnp.minimum(slot, NR * CAP - 1)])

        @pl.when(slot >= NR * CAP)
        def _():
            put(mine_ref[slot])

    incoming(n_vert, n_au, me_ref[0], info_ref, visit)
    out_ref[...] = pad_ref[:, :TS, :TS]


def window_kernel(n_vert, n_au, me_ref, info_ref, tile_ref, other_ref, taper_ref, model_ref, win_ref, pad_ref):
    total = tile_ref[...]
    for k in range(other_ref.shape[0]):
        total = total + other_ref[k]
    model = total * taper_ref[...][None]
    model_ref[...] = model
    pad_ref[:, :TS, :TS] = model
    pad_ref[:, :TS, TS:] = jnp.zeros((2, TS, 128), F32)
    pad_ref[:, TS:, :] = jnp.zeros((2, 8, TS + 128), F32)
    low = low_half((S, 2 * S))

    def visit(slot, row_at, col_at):
        top = pl.multiple_of(row_at // 8 * 8, 8)
        lift = lax.rem(S + 8 - row_at % 8, S + 8)
        start = pl.multiple_of(col_at // 128 * 128, 128)
        shift = lax.rem(256 - col_at % 128, 256)
        parts = []
        for plane in range(2):
            wide = pad_ref[plane, pl.ds(top, S + 8), pl.ds(start, 256)]
            wide = pltpu.roll(wide, shift, 1)[:, : 2 * S]
            parts.append(pltpu.roll(wide, lift, 0)[:S])
        win_ref[slot] = jnp.where(low, parts[0], pltpu.roll(parts[1], S, 1))

    incoming(n_vert, n_au, me_ref[0], info_ref, visit)


def degrid_kernel(me_ref, info_ref, where_ref, got_ref, mine_ref, aterm_ref, coord_ref, left_ref, right_ref,
                  out_ref, win_ref):
    rows = coord_ref.shape[1] // 2
    live = info_ref[me_ref[0], 5 * NB]
    out_ref[...] = jnp.zeros_like(out_ref)

    def step(b, _):
        slot = where_ref[b]

        @pl.when(slot < NR * CAP)
        def _():
            win_ref[...] = got_ref[jnp.minimum(slot, NR * CAP - 1)]

        @pl.when(slot >= NR * CAP)
        def _():
            win_ref[...] = mine_ref[slot]

        back = times(dft2(win_ref[...], left_ref[...], right_ref[...], True), aterm_ref[b], True)
        hi = back.astype(BF).astype(F32)
        both = jnp.concatenate([hi, back - hi], 0).T.astype(BF)
        at = pl.ds(b, 1)
        cu, su = phases(coord_ref[at, :rows])
        cv, sv = phases(coord_ref[at, rows:])
        ehi, elo = split(jnp.concatenate([cu, su], 1))
        m = jnp.dot(
            jnp.concatenate([both, both], 1),
            jnp.concatenate([ehi, ehi, elo, elo], 0),
            preferred_element_type=F32,
        )
        a_real = m[:S, :rows] + m[S:, rows:]
        a_imag = m[S:, :rows] - m[:S, rows:]
        real = jnp.sum(a_real * cv + a_imag * sv, axis=0, keepdims=True)
        imag = jnp.sum(a_imag * cv - a_real * sv, axis=0, keepdims=True)
        out_ref[at, :] = jnp.concatenate([real, imag], 1) * (1.0 / S)
        return 0

    lax.fori_loop(0, live, step, 0)


def beam_exchange_kernel(n_vert, cap, ids_ref, beam_ref, out_ref, send_ref, send_sem, recv_sem, own_sem):
    n = out_ref.shape[0]
    me = lax.axis_index("au") * n_vert + lax.axis_index("vert")
    barrier = pltpu.get_barrier_semaphore()

    def peer(k):
        t = lax.rem(me + k, n)
        return {"au": t // n_vert, "vert": t % n_vert}

    for k in range(1, n):
        pl.semaphore_signal(barrier, inc=1, device_id=peer(k), device_id_type=MESH)

    def fill(k, _):
        for j in range(cap):
            send_ref[k, j * S : (j + 1) * S, :] = beam_ref[ids_ref[k * cap + j]]
        return 0

    lax.fori_loop(0, n, fill, 0)
    own = pltpu.make_async_copy(send_ref.at[0], out_ref.at[0], own_sem)
    own.start()
    pl.semaphore_wait(barrier, n - 1)
    copies = []
    for k in range(1, n):
        copies.append(pltpu.make_async_remote_copy(
            send_ref.at[k], out_ref.at[k], send_sem.at[k], recv_sem.at[k],
            device_id=peer(k), device_id_type=MESH))
        copies[-1].start()
    own.wait()
    for copy in copies:
        copy.wait()


def route_kernel(n_au, n_vert, sign, in_ref, out_ref, send_sem, recv_sem):
    row, col = lax.axis_index("au"), lax.axis_index("vert")
    barrier = pltpu.get_barrier_semaphore()

    def inside(dr, dc):
        return (row + dr >= 0) & (row + dr < n_au) & (col + dc >= 0) & (col + dc < n_vert)

    for dr, dc in ROUTES:
        @pl.when(inside(dr, dc))
        def _():
            pl.semaphore_signal(barrier, inc=1, device_id={"au": row + dr, "vert": col + dc},
                                device_id_type=MESH)
    tall = 1 + jnp.minimum(row, 1) + jnp.minimum(n_au - 1 - row, 1)
    wide = 1 + jnp.minimum(col, 1) + jnp.minimum(n_vert - 1 - col, 1)
    pl.semaphore_wait(barrier, tall * wide - 1)

    def copy_of(i, dr, dc):
        at = pl.ds(i * CAP, CAP)
        return pltpu.make_async_remote_copy(
            in_ref.at[at], out_ref.at[at], send_sem.at[i], recv_sem.at[i],
            device_id={"au": row + dr, "vert": col + dc}, device_id_type=MESH)

    for i, (dr, dc) in enumerate(ROUTES):
        dr, dc = sign * dr, sign * dc

        @pl.when(inside(dr, dc))
        def _():
            copy_of(i, dr, dc).start()
    for i, (dr, dc) in enumerate(ROUTES):
        dr, dc = sign * dr, sign * dc

        @pl.when(inside(dr, dc))
        def _():
            copy_of(i, dr, dc).wait_send()

        @pl.when(inside(-dr, -dc))
        def _():
            copy_of(i, dr, dc).wait_recv()


def tile_exchange_kernel(in_ref, out_ref, send_sem, recv_sem):
    n = out_ref.shape[0] + 1
    me = lax.axis_index("af")
    barrier = pltpu.get_barrier_semaphore()
    for k in range(1, n):
        pl.semaphore_signal(barrier, inc=1, device_id={"af": lax.rem(me + k, n)}, device_id_type=MESH)
    pl.semaphore_wait(barrier, n - 1)
    copies = []
    for k in range(1, n):
        copies.append(pltpu.make_async_remote_copy(
            in_ref, out_ref.at[k - 1], send_sem.at[k - 1], recv_sem.at[k - 1],
            device_id={"af": lax.rem(me + k, n)}, device_id_type=MESH))
        copies[-1].start()
    for copy in copies:
        copy.wait()


SMEM = pl.BlockSpec(memory_space=pltpu.SMEM)
VMEM = pl.BlockSpec(memory_space=pltpu.VMEM)
ANY = pl.BlockSpec(memory_space=pl.ANY)


def shape(*dims, dtype=F32):
    return jax.ShapeDtypeStruct(dims, dtype)


def local_call(kernel, in_specs, out_specs, out_shape, scratch=()):
    return pl.pallas_call(
        kernel, in_specs=in_specs, out_specs=out_specs, out_shape=out_shape,
        scratch_shapes=list(scratch),
        compiler_params=pltpu.CompilerParams(vmem_limit_bytes=VMEM_LIMIT))


def remote_call(kernel, ident, in_specs, out_shape, scratch):
    return pl.pallas_call(
        kernel, in_specs=in_specs, out_specs=ANY, out_shape=out_shape, scratch_shapes=scratch,
        compiler_params=pltpu.CompilerParams(
            collective_id=ident, has_side_effects=True, vmem_limit_bytes=VMEM_LIMIT))


def body(visib, coords, owner, offsets, stations, live, beams, taper):
    n_au, n_vert, n_af = lax.axis_size("au"), lax.axis_size("vert"), lax.axis_size("af")
    n = n_au * n_vert
    per_dev = beams.shape[1]
    cap = 2 * NB // n + 2
    me = lax.axis_index("au") * n_vert + lax.axis_index("vert")
    mine = me.astype(jnp.int32).reshape(1)
    signal, places = visib[0], coords[0]
    rows2 = signal.shape[1]
    info = jnp.concatenate(
        [owner[0], offsets[0, :, 0], offsets[0, :, 1], stations[0, :, 0], stations[0, :, 1],
         jnp.broadcast_to(live[0, 0], (128 - 5 * NB,))])
    info = lax.all_gather(info, ("au", "vert"), axis=0)
    left, right, right_conj = constants()

    images = local_call(image_kernel, [VMEM] * 2, VMEM, shape(NB, S, 2 * S))(signal, places)

    asked = jnp.roll(info[:, 3 * NB : 5 * NB], -me, axis=0).reshape(n, 2, NB)
    asked = asked.transpose(0, 2, 1).reshape(n, 2 * NB)
    hit = asked // per_dev == me
    entry = jnp.arange(2 * NB, dtype=jnp.int32)
    order = jnp.sum((hit[:, None, :] & (entry[None, :] < entry[:, None])[None]).astype(jnp.int32), axis=2)
    pick = hit[:, None, :] & (order[:, None, :] == jnp.arange(cap, dtype=jnp.int32)[None, :, None])
    ids = jnp.sum(jnp.where(pick, (asked % per_dev)[:, None, :], 0), axis=2).reshape(n * cap)
    found = remote_call(
        lambda *refs: beam_exchange_kernel(n_vert, cap, *refs), 1, [SMEM, VMEM],
        shape(n, cap * S, 2 * S, dtype=BF),
        [pltpu.VMEM((n, cap * S, 2 * S), BF), pltpu.SemaphoreType.DMA((n,)),
         pltpu.SemaphoreType.DMA((n,)), pltpu.SemaphoreType.DMA],
    )(ids, beams[0].reshape(per_dev, S, 2 * S))

    subgrids, aterms, slots = local_call(
        lambda *refs: subgrid_kernel(n_vert, per_dev, cap, *refs),
        [SMEM, SMEM] + [VMEM] * 4, [VMEM, VMEM, SMEM],
        [shape(NSLOT, S, 2 * S), shape(NB, S, 2 * S), shape(NB, dtype=jnp.int32)],
        [pltpu.SMEM((n,), jnp.int32), pltpu.SMEM((9,), jnp.int32)],
    )(mine, info, images, found.reshape(n * cap, S, 2 * S), left, right)

    def routed(values, sign, ident):
        return remote_call(
            lambda *refs: route_kernel(n_au, n_vert, sign, *refs), ident, [ANY],
            shape(NR * CAP, S, 2 * S),
            [pltpu.SemaphoreType.DMA((NR,)), pltpu.SemaphoreType.DMA((NR,))])(values)

    arrived = routed(subgrids, 1, 2)
    tile = local_call(
        lambda *refs: tile_kernel(n_vert, n_au, *refs), [SMEM, SMEM, VMEM, VMEM], VMEM,
        shape(2, TS, TS), [pltpu.VMEM((2, TS + 8, TS + 128), F32)])(mine, info, arrived, subgrids)
    others = remote_call(
        tile_exchange_kernel, 3, [ANY], shape(n_af - 1, 2, TS, TS),
        [pltpu.SemaphoreType.DMA((n_af - 1,)), pltpu.SemaphoreType.DMA((n_af - 1,))])(tile)
    model_grid, windows = local_call(
        lambda *refs: window_kernel(n_vert, n_au, *refs), [SMEM, SMEM] + [VMEM] * 3, [VMEM, VMEM],
        [shape(2, TS, TS), shape(NSLOT, S, 2 * S)], [pltpu.VMEM((2, TS + 8, TS + 128), F32)],
    )(mine, info, tile, others, taper)
    returned = routed(windows, -1, 4)
    result = local_call(
        degrid_kernel, [SMEM] * 3 + [VMEM] * 6, VMEM, shape(NB, rows2), [pltpu.VMEM((S, 2 * S), F32)],
    )(mine, info, slots, returned, windows, aterms, places, left, right_conj)
    return (result[None], model_grid)


def solution(mesh):
    placed = (
        P("af", ("au", "vert"), None),
        P("af", ("au", "vert"), None),
        P("af", ("au", "vert")),
        P("af", ("au", "vert"), None),
        P("af", ("au", "vert"), None),
        P("af", ("au", "vert")),
        P("af", ("au", "vert"), None),
        P("au", "vert"),
    )
    return jax.shard_map(
        body,
        mesh=mesh,
        in_specs=placed,
        out_specs=(P("af", ("au", "vert"), None), P(None, "au", "vert")),
        check_vma=False,
    )
```

```python
import math

import jax
import jax.numpy as jnp
import numpy as np
from jax import lax
from jax.experimental import pallas as pl
from jax.experimental.pallas import tpu as pltpu
from jax.sharding import PartitionSpec as P

S = 64
CAP = 2
NB = 16
TS = 512
BF = jnp.bfloat16
F32 = jnp.float32
MESH = pl.DeviceIdType.MESH
ROUTES = tuple((r, c) for r in (-1, 0, 1) for c in (-1, 0, 1) if (r, c) != (0, 0))
NR = len(ROUTES)
NSLOT = NR * CAP + NB
VMEM_LIMIT = 32 * 1024 * 1024


def fit(fn, count):
    k = np.arange(400)
    z = 0.125 * (1.0 + np.cos(np.pi * (k + 0.5) / 400))
    cheb = np.polynomial.chebyshev.Chebyshev.fit(z, fn(np.sqrt(z)), count - 1, domain=[0, 0.25])
    return [float(v) for v in cheb.convert(kind=np.polynomial.Polynomial).coef]


COS = fit(lambda t: np.cos(2 * np.pi * t), 8)
SIN = fit(lambda t: np.sin(2 * np.pi * t) / t, 8)


def dft_tables():
    pos = np.arange(S)
    ang = (pos[:, None] * pos[None, :] % S) * (2.0 * np.pi / S)
    return np.cos(ang) / math.sqrt(S), -np.sin(ang) / math.sqrt(S)


def split_np(x):
    x = x.astype(np.float32)
    hi = x.astype(BF).astype(np.float32)
    return hi, (x - hi).astype(BF).astype(np.float32)


def constants():
    fr, fi = dft_tables()
    hi, lo = split_np(np.concatenate([fr, fi], 0))
    left = np.concatenate([hi, hi, lo, lo], 1)
    out = [left]
    for sign in (1, -1):
        right = np.concatenate(
            [np.concatenate([fr, sign * fi], 1), np.concatenate([-sign * fi, fr], 1)], 0
        )
        hi, lo = split_np(right)
        out.append(np.concatenate([np.concatenate([hi, hi], 0), np.concatenate([lo, lo], 0)], 1))
    return [v.astype(BF) for v in out]


def split(x):
    hi = x.astype(BF)
    return hi, (x - hi.astype(F32)).astype(BF)


def horner(coefs, z):
    acc = jnp.full(z.shape, coefs[-1], F32)
    for c in coefs[-2::-1]:
        acc = acc * z + c
    return acc


def cos_sin(turns):
    t = turns - jnp.round(turns)
    z = t * t
    return horner(COS, z), horner(SIN, z) * t


def phases(u):
    j = lax.broadcasted_iota(jnp.int32, (8, u.shape[1]), 0).astype(F32)
    c1, s1 = cos_sin(u * (j * (1.0 / 64)))
    c2, s2 = cos_sin(u * (j * 0.125 - 0.5))
    cs, ss = [], []
    for k in range(8):
        ck, sk = c2[k : k + 1], s2[k : k + 1]
        cs.append(ck * c1 - sk * s1)
        ss.append(sk * c1 + ck * s1)
    return jnp.concatenate(cs, 0), jnp.concatenate(ss, 0)


def low_half(shape):
    return lax.broadcasted_iota(jnp.int32, shape, 1) < S


def rotate(x):
    y = pltpu.roll(x, S, 1)
    return jnp.where(low_half(x.shape), -y, y)


def times(x, a, conj):
    low = low_half(x.shape)
    ra = pltpu.roll(a, S, 1)
    rr = jnp.where(low, a, ra)
    ii = jnp.where(low, ra, a)
    y = pltpu.roll(x, S, 1) * ii
    sgn = low if conj else jnp.logical_not(low)
    return x * rr + jnp.where(sgn, y, -y)


def dft2(blocks, left, right, conj):
    width = 2 * S
    hi, lo = split(jnp.concatenate(blocks, 1) if len(blocks) > 1 else blocks[0])
    m = jnp.dot(left, jnp.concatenate([hi, lo, hi, lo], 0), preferred_element_type=F32)
    rows = []
    for i in range(len(blocks)):
        part = m[:, i * width : (i + 1) * width]
        turned = rotate(part[S:])
        rows.append(part[:S] - turned if conj else part[:S] + turned)
    hi, lo = split(jnp.concatenate(rows, 0))
    m = jnp.dot(jnp.concatenate([hi, lo], 1), right, preferred_element_type=F32)
    m = m[:, :width] + m[:, width:]
    return [m[i * S : (i + 1) * S] for i in range(len(blocks))]


def make_images(vis_ref, coord_ref, out_ref):
    rows = vis_ref.shape[1] // 2

    def step(b, _):
        at = pl.ds(b, 1)
        cu, su = phases(coord_ref[at, :rows])
        cv, sv = phases(coord_ref[at, rows:])
        vr, vi = vis_ref[at, :rows], vis_ref[at, rows:]
        ahi, alo = split(jnp.concatenate([cu, su], 0))
        bhi, blo = split(jnp.concatenate([vr * cv - vi * sv, vr * sv + vi * cv], 0))
        m = lax.dot_general(
            jnp.concatenate([ahi, alo], 0),
            jnp.concatenate([bhi, blo], 0),
            (((1,), (1,)), ((), ())),
            preferred_element_type=F32,
        )
        m = m[: 2 * S] + m[2 * S :]
        m = m[:, : 2 * S] + m[:, 2 * S :]
        out_ref[b] = (m[:S] + rotate(m[S:])) * (1.0 / math.sqrt(rows))
        return 0

    lax.fori_loop(0, NB, step, 0)


def subgrid_kernel(n_vert, per_dev, cap, me_ref, info_ref, image_ref, beam_ref, left_ref, right_ref,
                   out_ref, aterm_ref, where_ref, count_ref, heads_ref):
    me = me_ref[0]
    n = info_ref.shape[0]
    row, col = me // n_vert, me % n_vert

    def zero(i, _):
        count_ref[i] = 0
        return 0

    lax.fori_loop(0, n, zero, 0)
    for i in range(9):
        heads_ref[i] = 0
    live = info_ref[me, 5 * NB]

    def find(station):
        keeper = station // per_dev
        order = count_ref[keeper]
        count_ref[keeper] = order + 1
        return lax.rem(me - keeper + n, n) * cap + order

    def place(b):
        first = find(info_ref[me, 3 * NB + b])
        second = find(info_ref[me, 4 * NB + b])
        owner = info_ref[me, b]
        head = (owner // n_vert - row + 1) * 3 + (owner % n_vert - col + 1)
        head = jnp.where(b < live, head, 4)
        order = heads_ref[head]
        heads_ref[head] = order + 1
        slot = jnp.where(head == 4, NR * CAP + b, jnp.where(head < 4, head, head - 1) * CAP + order)
        where_ref[b] = slot
        return first, second, slot

    def step(i, _):
        places = [place(i * 4 + j) for j in range(4)]
        blocks = []
        for j in range(4):
            p = beam_ref[places[j][0]].astype(F32)
            q = beam_ref[places[j][1]].astype(F32)
            aterm = times(p, q, True)
            aterm_ref[i * 4 + j] = aterm
            blocks.append(times(image_ref[i * 4 + j], aterm, False))
        blocks = dft2(blocks, left_ref[...], right_ref[...], False)
        for j in range(4):
            out_ref[places[j][2]] = blocks[j]
        return 0

    lax.fori_loop(0, NB // 4, step, 0)


def incoming(n_vert, n_au, me, info_ref, visit):
    row, col = me // n_vert, me % n_vert
    for route, (dr, dc) in enumerate(ROUTES):
        sr, sc = row - dr, col - dc
        inside = (sr >= 0) & (sr < n_au) & (sc >= 0) & (sc < n_vert)

        @pl.when(inside)
        def _(route=route, src=sr * n_vert + sc):
            live = info_ref[src, 5 * NB]

            def look(b, count):
                hit = info_ref[src, b] == me

                @pl.when(hit)
                def _():
                    visit(route * CAP + count, info_ref[src, NB + b], info_ref[src, 2 * NB + b])

                return count + hit.astype(jnp.int32)

            lax.fori_loop(0, live, look, jnp.int32(0))

    def own(b, _):
        @pl.when(info_ref[me, b] == me)
        def _():
            visit(NR * CAP + b, info_ref[me, NB + b], info_ref[me, 2 * NB + b])

        return 0

    lax.fori_loop(0, info_ref[me, 5 * NB], own, 0)


def tile_kernel(n_vert, n_au, me_ref, info_ref, got_ref, mine_ref, out_ref, pad_ref):
    pad_ref[...] = jnp.zeros_like(pad_ref)
    low = low_half((S, 2 * S))
    blank = jnp.zeros((S, 2 * S), F32)
    blank_rows = jnp.zeros((8, 256), F32)

    def visit(slot, row_at, col_at):
        top = pl.multiple_of(row_at // 8 * 8, 8)
        start = pl.multiple_of(col_at // 128 * 128, 128)
        shift = col_at % 128

        def put(x):
            for plane in range(2):
                part = x if plane == 0 else pltpu.roll(x, S, 1)
                wide = jnp.concatenate([jnp.where(low, part, 0.0), blank], 1)
                wide = jnp.concatenate([pltpu.roll(wide, shift, 1), blank_rows], 0)
                at = (plane, pl.ds(top, S + 8), pl.ds(start, 256))
                pad_ref[at] += pltpu.roll(wide, row_at % 8, 0)

        @pl.when(slot < NR * CAP)
        def _():
            put(got_ref[jnp.minimum(slot, NR * CAP - 1)])

        @pl.when(slot >= NR * CAP)
        def _():
            put(mine_ref[slot])

    incoming(n_vert, n_au, me_ref[0], info_ref, visit)
    out_ref[...] = pad_ref[:, :TS, :TS]


def window_kernel(n_vert, n_au, me_ref, info_ref, tile_ref, other_ref, taper_ref, model_ref, win_ref, pad_ref):
    total = tile_ref[...]
    for k in range(other_ref.shape[0]):
        total = total + other_ref[k]
    model = total * taper_ref[...][None]
    model_ref[...] = model
    pad_ref[:, :TS, :TS] = model
    pad_ref[:, :TS, TS:] = jnp.zeros((2, TS, 128), F32)
    pad_ref[:, TS:, :] = jnp.zeros((2, 8, TS + 128), F32)
    low = low_half((S, 2 * S))

    def visit(slot, row_at, col_at):
        top = pl.multiple_of(row_at // 8 * 8, 8)
        lift = lax.rem(S + 8 - row_at % 8, S + 8)
        start = pl.multiple_of(col_at // 128 * 128, 128)
        shift = lax.rem(256 - col_at % 128, 256)
        parts = []
        for plane in range(2):
            wide = pad_ref[plane, pl.ds(top, S + 8), pl.ds(start, 256)]
            wide = pltpu.roll(wide, shift, 1)[:, : 2 * S]
            parts.append(pltpu.roll(wide, lift, 0)[:S])
        win_ref[slot] = jnp.where(low, parts[0], pltpu.roll(parts[1], S, 1))

    incoming(n_vert, n_au, me_ref[0], info_ref, visit)


def degrid_kernel(me_ref, info_ref, where_ref, got_ref, mine_ref, aterm_ref, coord_ref, left_ref, right_ref,
                  out_ref, win_ref):
    rows = coord_ref.shape[1] // 2
    live = info_ref[me_ref[0], 5 * NB]

    def fetch(b, _):
        slot = where_ref[b]

        @pl.when(slot < NR * CAP)
        def _():
            win_ref[b] = got_ref[jnp.minimum(slot, NR * CAP - 1)]

        @pl.when(slot >= NR * CAP)
        def _():
            win_ref[b] = mine_ref[slot]

        return 0

    lax.fori_loop(0, NB, fetch, 0)

    def transform(i, _):
        blocks = [win_ref[i * 4 + j] for j in range(4)]
        blocks = dft2(blocks, left_ref[...], right_ref[...], True)
        for j in range(4):
            win_ref[i * 4 + j] = times(blocks[j], aterm_ref[i * 4 + j], True)
        return 0

    lax.fori_loop(0, NB // 4, transform, 0)

    def predict(b):
        back = win_ref[b]
        hi = back.astype(BF).astype(F32)
        both = jnp.concatenate([hi, back - hi], 0).T.astype(BF)
        at = pl.ds(b, 1)
        cu, su = phases(coord_ref[at, :rows])
        cv, sv = phases(coord_ref[at, rows:])
        ehi, elo = split(jnp.concatenate([cu, su], 1))
        m = jnp.dot(
            jnp.concatenate([both, both], 1),
            jnp.concatenate([ehi, ehi, elo, elo], 0),
            preferred_element_type=F32,
        )
        a_real = m[:S, :rows] + m[S:, rows:]
        a_imag = m[S:, :rows] - m[:S, rows:]
        real = jnp.sum(a_real * cv + a_imag * sv, axis=0, keepdims=True)
        imag = jnp.sum(a_imag * cv - a_real * sv, axis=0, keepdims=True)
        return jnp.concatenate([real, imag], 1) * (1.0 / S)

    def step(i, _):
        found = [predict(i * 2 + j) for j in range(2)]
        for j in range(2):
            out_ref[pl.ds(i * 2 + j, 1), :] = jnp.where(i * 2 + j < live, found[j], 0.0)
        return 0

    lax.fori_loop(0, NB // 2, step, 0)


def info_kernel(n_vert, in_ref, out_ref, send_sem, recv_sem, own_sem):
    n = out_ref.shape[0]
    me = lax.axis_index("au") * n_vert + lax.axis_index("vert")
    barrier = pltpu.get_barrier_semaphore()

    def peer(k):
        t = lax.rem(me + k, n)
        return {"au": t // n_vert, "vert": t % n_vert}

    for k in range(1, n):
        pl.semaphore_signal(barrier, inc=1, device_id=peer(k), device_id_type=MESH)
    own = pltpu.make_async_copy(in_ref, out_ref.at[me], own_sem)
    own.start()
    pl.semaphore_wait(barrier, n - 1)
    copies = []
    for k in range(1, n):
        copies.append(pltpu.make_async_remote_copy(
            in_ref, out_ref.at[me], send_sem.at[k], recv_sem.at[k],
            device_id=peer(k), device_id_type=MESH))
        copies[-1].start()
    own.wait()
    for copy in copies:
        copy.wait()


def beam_exchange_kernel(n_vert, cap, ids_ref, beam_ref, vis_ref, coord_ref, out_ref, image_ref,
                         send_ref, send_sem, recv_sem, own_sem):
    n = out_ref.shape[0]
    me = lax.axis_index("au") * n_vert + lax.axis_index("vert")
    barrier = pltpu.get_barrier_semaphore()

    def peer(k):
        t = lax.rem(me + k, n)
        return {"au": t // n_vert, "vert": t % n_vert}

    for k in range(1, n):
        pl.semaphore_signal(barrier, inc=1, device_id=peer(k), device_id_type=MESH)

    def fill(k, _):
        for j in range(cap):
            send_ref[k, j * S : (j + 1) * S, :] = beam_ref[ids_ref[k * cap + j]]
        return 0

    lax.fori_loop(0, n, fill, 0)
    own = pltpu.make_async_copy(send_ref.at[0], out_ref.at[0], own_sem)
    own.start()
    pl.semaphore_wait(barrier, n - 1)
    copies = []
    for k in range(1, n):
        copies.append(pltpu.make_async_remote_copy(
            send_ref.at[k], out_ref.at[k], send_sem.at[k], recv_sem.at[k],
            device_id=peer(k), device_id_type=MESH))
        copies[-1].start()
    make_images(vis_ref, coord_ref, image_ref)
    own.wait()
    for copy in copies:
        copy.wait()


def route_kernel(n_au, n_vert, sign, in_ref, out_ref, send_sem, recv_sem):
    row, col = lax.axis_index("au"), lax.axis_index("vert")
    barrier = pltpu.get_barrier_semaphore()

    def inside(dr, dc):
        return (row + dr >= 0) & (row + dr < n_au) & (col + dc >= 0) & (col + dc < n_vert)

    for dr, dc in ROUTES:
        @pl.when(inside(dr, dc))
        def _():
            pl.semaphore_signal(barrier, inc=1, device_id={"au": row + dr, "vert": col + dc},
                                device_id_type=MESH)
    tall = 1 + jnp.minimum(row, 1) + jnp.minimum(n_au - 1 - row, 1)
    wide = 1 + jnp.minimum(col, 1) + jnp.minimum(n_vert - 1 - col, 1)
    pl.semaphore_wait(barrier, tall * wide - 1)

    def copy_of(i, dr, dc):
        at = pl.ds(i * CAP, CAP)
        return pltpu.make_async_remote_copy(
            in_ref.at[at], out_ref.at[at], send_sem.at[i], recv_sem.at[i],
            device_id={"au": row + dr, "vert": col + dc}, device_id_type=MESH)

    for i, (dr, dc) in enumerate(ROUTES):
        dr, dc = sign * dr, sign * dc

        @pl.when(inside(dr, dc))
        def _():
            copy_of(i, dr, dc).start()
    for i, (dr, dc) in enumerate(ROUTES):
        dr, dc = sign * dr, sign * dc

        @pl.when(inside(dr, dc))
        def _():
            copy_of(i, dr, dc).wait_send()

        @pl.when(inside(-dr, -dc))
        def _():
            copy_of(i, dr, dc).wait_recv()


def tile_exchange_kernel(in_ref, out_ref, send_sem, recv_sem):
    n = out_ref.shape[0] + 1
    me = lax.axis_index("af")
    barrier = pltpu.get_barrier_semaphore()
    for k in range(1, n):
        pl.semaphore_signal(barrier, inc=1, device_id={"af": lax.rem(me + k, n)}, device_id_type=MESH)
    pl.semaphore_wait(barrier, n - 1)
    copies = []
    for k in range(1, n):
        copies.append(pltpu.make_async_remote_copy(
            in_ref, out_ref.at[k - 1], send_sem.at[k - 1], recv_sem.at[k - 1],
            device_id={"af": lax.rem(me + k, n)}, device_id_type=MESH))
        copies[-1].start()
    for copy in copies:
        copy.wait()


SMEM = pl.BlockSpec(memory_space=pltpu.SMEM)
VMEM = pl.BlockSpec(memory_space=pltpu.VMEM)
ANY = pl.BlockSpec(memory_space=pl.ANY)


def shape(*dims, dtype=F32):
    return jax.ShapeDtypeStruct(dims, dtype)


def local_call(kernel, in_specs, out_specs, out_shape, scratch=()):
    return pl.pallas_call(
        kernel, in_specs=in_specs, out_specs=out_specs, out_shape=out_shape,
        scratch_shapes=list(scratch),
        compiler_params=pltpu.CompilerParams(vmem_limit_bytes=VMEM_LIMIT))


def remote_call(kernel, ident, in_specs, out_shape, scratch, out_specs=ANY):
    return pl.pallas_call(
        kernel, in_specs=in_specs, out_specs=out_specs, out_shape=out_shape, scratch_shapes=scratch,
        compiler_params=pltpu.CompilerParams(
            collective_id=ident, has_side_effects=True, vmem_limit_bytes=VMEM_LIMIT))


def body(visib, coords, owner, offsets, stations, live, beams, taper):
    n_au, n_vert, n_af = lax.axis_size("au"), lax.axis_size("vert"), lax.axis_size("af")
    n = n_au * n_vert
    per_dev = beams.shape[1]
    cap = 2 * NB // n + 2
    me = lax.axis_index("au") * n_vert + lax.axis_index("vert")
    mine = me.astype(jnp.int32).reshape(1)
    signal, places = visib[0], coords[0]
    rows2 = signal.shape[1]
    info = jnp.concatenate(
        [owner[0], offsets[0, :, 0], offsets[0, :, 1], stations[0, :, 0], stations[0, :, 1],
         jnp.broadcast_to(live[0, 0], (128 - 5 * NB,))])
    info = remote_call(
        lambda *refs: info_kernel(n_vert, *refs), 5, [VMEM], shape(n, 1, 128, dtype=jnp.int32),
        [pltpu.SemaphoreType.DMA((n,)), pltpu.SemaphoreType.DMA((n,)), pltpu.SemaphoreType.DMA],
        out_specs=VMEM,
    )(info.reshape(1, 128)).reshape(n, 128)
    left, right, right_conj = constants()

    asked = jnp.roll(info[:, 3 * NB : 5 * NB], -me, axis=0).reshape(n, 2, NB)
    asked = asked.transpose(0, 2, 1).reshape(n, 2 * NB)
    hit = asked // per_dev == me
    entry = jnp.arange(2 * NB, dtype=jnp.int32)
    order = jnp.sum((hit[:, None, :] & (entry[None, :] < entry[:, None])[None]).astype(jnp.int32), axis=2)
    pick = hit[:, None, :] & (order[:, None, :] == jnp.arange(cap, dtype=jnp.int32)[None, :, None])
    ids = jnp.sum(jnp.where(pick, (asked % per_dev)[:, None, :], 0), axis=2).reshape(n * cap)
    found, images = remote_call(
        lambda *refs: beam_exchange_kernel(n_vert, cap, *refs), 1, [SMEM] + [VMEM] * 3,
        [shape(n, cap * S, 2 * S, dtype=BF), shape(NB, S, 2 * S)],
        [pltpu.VMEM((n, cap * S, 2 * S), BF), pltpu.SemaphoreType.DMA((n,)),
         pltpu.SemaphoreType.DMA((n,)), pltpu.SemaphoreType.DMA],
        out_specs=[ANY, VMEM],
    )(ids, beams[0].reshape(per_dev, S, 2 * S), signal, places)

    subgrids, aterms, slots = local_call(
        lambda *refs: subgrid_kernel(n_vert, per_dev, cap, *refs),
        [SMEM, SMEM] + [VMEM] * 4, [VMEM, VMEM, SMEM],
        [shape(NSLOT, S, 2 * S), shape(NB, S, 2 * S), shape(NB, dtype=jnp.int32)],
        [pltpu.SMEM((n,), jnp.int32), pltpu.SMEM((9,), jnp.int32)],
    )(mine, info, images, found.reshape(n * cap, S, 2 * S), left, right)

    def routed(values, sign, ident):
        return remote_call(
            lambda *refs: route_kernel(n_au, n_vert, sign, *refs), ident, [ANY],
            shape(NR * CAP, S, 2 * S),
            [pltpu.SemaphoreType.DMA((NR,)), pltpu.SemaphoreType.DMA((NR,))])(values)

    arrived = routed(subgrids, 1, 2)
    tile = local_call(
        lambda *refs: tile_kernel(n_vert, n_au, *refs), [SMEM, SMEM, VMEM, VMEM], VMEM,
        shape(2, TS, TS), [pltpu.VMEM((2, TS + 8, TS + 128), F32)])(mine, info, arrived, subgrids)
    others = remote_call(
        tile_exchange_kernel, 3, [ANY], shape(n_af - 1, 2, TS, TS),
        [pltpu.SemaphoreType.DMA((n_af - 1,)), pltpu.SemaphoreType.DMA((n_af - 1,))])(tile)
    model_grid, windows = local_call(
        lambda *refs: window_kernel(n_vert, n_au, *refs), [SMEM, SMEM] + [VMEM] * 3, [VMEM, VMEM],
        [shape(2, TS, TS), shape(NSLOT, S, 2 * S)], [pltpu.VMEM((2, TS + 8, TS + 128), F32)],
    )(mine, info, tile, others, taper)
    returned = routed(windows, -1, 4)
    result = local_call(
        degrid_kernel, [SMEM] * 3 + [VMEM] * 6, VMEM, shape(NB, rows2), [pltpu.VMEM((NB, S, 2 * S), F32)],
    )(mine, info, slots, returned, windows, aterms, places, left, right_conj)
    return (result[None], model_grid)


def solution(mesh):
    placed = (
        P("af", ("au", "vert"), None),
        P("af", ("au", "vert"), None),
        P("af", ("au", "vert")),
        P("af", ("au", "vert"), None),
        P("af", ("au", "vert"), None),
        P("af", ("au", "vert")),
        P("af", ("au", "vert"), None),
        P("au", "vert"),
    )
    return jax.shard_map(
        body,
        mesh=mesh,
        in_specs=placed,
        out_specs=(P("af", ("au", "vert"), None), P(None, "au", "vert")),
        check_vma=False,
    )
```

```python
import math

import jax
import jax.numpy as jnp
import numpy as np
from jax import lax
from jax.experimental import pallas as pl
from jax.experimental.pallas import tpu as pltpu
from jax.sharding import PartitionSpec as P

S = 64
CAP = 2
NB = 16
TS = 512
BF = jnp.bfloat16
F32 = jnp.float32
MESH = pl.DeviceIdType.MESH
ROUTES = tuple((r, c) for r in (-1, 0, 1) for c in (-1, 0, 1) if (r, c) != (0, 0))
NR = len(ROUTES)
NSLOT = NR * CAP + NB
VMEM_LIMIT = 32 * 1024 * 1024


def fit(fn, count):
    k = np.arange(400)
    z = 0.125 * (1.0 + np.cos(np.pi * (k + 0.5) / 400))
    cheb = np.polynomial.chebyshev.Chebyshev.fit(z, fn(np.sqrt(z)), count - 1, domain=[0, 0.25])
    return [float(v) for v in cheb.convert(kind=np.polynomial.Polynomial).coef]


COS = fit(lambda t: np.cos(2 * np.pi * t), 8)
SIN = fit(lambda t: np.sin(2 * np.pi * t) / t, 8)


def dft_tables():
    pos = np.arange(S)
    ang = (pos[:, None] * pos[None, :] % S) * (2.0 * np.pi / S)
    return np.cos(ang) / math.sqrt(S), -np.sin(ang) / math.sqrt(S)


def split_np(x):
    x = x.astype(np.float32)
    hi = x.astype(BF).astype(np.float32)
    return hi, (x - hi).astype(BF).astype(np.float32)


def constants():
    fr, fi = dft_tables()
    hi, lo = split_np(np.concatenate([fr, fi], 0))
    left = np.concatenate([hi, hi, lo, lo], 1)
    out = [left]
    for sign in (1, -1):
        right = np.concatenate(
            [np.concatenate([fr, sign * fi], 1), np.concatenate([-sign * fi, fr], 1)], 0
        )
        hi, lo = split_np(right)
        out.append(np.concatenate([np.concatenate([hi, hi], 0), np.concatenate([lo, lo], 0)], 1))
    return [v.astype(BF) for v in out]


def split(x):
    hi = x.astype(BF)
    return hi, (x - hi.astype(F32)).astype(BF)


def horner(coefs, z):
    acc = jnp.full(z.shape, coefs[-1], F32)
    for c in coefs[-2::-1]:
        acc = acc * z + c
    return acc


def cos_sin(turns):
    t = turns - jnp.round(turns)
    z = t * t
    return horner(COS, z), horner(SIN, z) * t


def phases(u):
    j = lax.broadcasted_iota(jnp.int32, (8, u.shape[1]), 0).astype(F32)
    c1, s1 = cos_sin(u * (j * (1.0 / 64)))
    c2, s2 = cos_sin(u * (j * 0.125 - 0.5))
    cs, ss = [], []
    for k in range(8):
        ck, sk = c2[k : k + 1], s2[k : k + 1]
        cs.append(ck * c1 - sk * s1)
        ss.append(sk * c1 + ck * s1)
    return jnp.concatenate(cs, 0), jnp.concatenate(ss, 0)


def low_half(shape):
    return lax.broadcasted_iota(jnp.int32, shape, 1) < S


def rotate(x):
    y = pltpu.roll(x, S, 1)
    return jnp.where(low_half(x.shape), -y, y)


def times(x, a, conj):
    low = low_half(x.shape)
    ra = pltpu.roll(a, S, 1)
    rr = jnp.where(low, a, ra)
    ii = jnp.where(low, ra, a)
    y = pltpu.roll(x, S, 1) * ii
    sgn = low if conj else jnp.logical_not(low)
    return x * rr + jnp.where(sgn, y, -y)


def dft2(blocks, left, right, conj):
    width = 2 * S
    hi, lo = split(jnp.concatenate(blocks, 1) if len(blocks) > 1 else blocks[0])
    m = jnp.dot(left, jnp.concatenate([hi, lo, hi, lo], 0), preferred_element_type=F32)
    rows = []
    for i in range(len(blocks)):
        part = m[:, i * width : (i + 1) * width]
        turned = rotate(part[S:])
        rows.append(part[:S] - turned if conj else part[:S] + turned)
    hi, lo = split(jnp.concatenate(rows, 0))
    m = jnp.dot(jnp.concatenate([hi, lo], 1), right, preferred_element_type=F32)
    m = m[:, :width] + m[:, width:]
    return [m[i * S : (i + 1) * S] for i in range(len(blocks))]


def make_images(vis_ref, coord_ref, out_ref, wave_ref, trig_ref):
    rows = vis_ref.shape[1] // 2

    def step(b, _):
        at = pl.ds(b, 1)
        cu, su = phases(coord_ref[at, :rows])
        cv, sv = phases(coord_ref[at, rows:])
        vr, vi = vis_ref[at, :rows], vis_ref[at, rows:]
        trig_ref[b, :S] = cv
        trig_ref[b, S:] = sv
        ahi, alo = split(jnp.concatenate([cu, su], 0))
        wave_ref[b, :S, :rows] = ahi[:S]
        wave_ref[b, :S, rows:] = ahi[S:]
        wave_ref[b, S:, :rows] = alo[:S]
        wave_ref[b, S:, rows:] = alo[S:]
        bhi, blo = split(jnp.concatenate([vr * cv - vi * sv, vr * sv + vi * cv], 0))
        m = lax.dot_general(
            jnp.concatenate([ahi, alo], 0),
            jnp.concatenate([bhi, blo], 0),
            (((1,), (1,)), ((), ())),
            preferred_element_type=F32,
        )
        m = m[: 2 * S] + m[2 * S :]
        m = m[:, : 2 * S] + m[:, 2 * S :]
        out_ref[b] = (m[:S] + rotate(m[S:])) * (1.0 / math.sqrt(rows))
        return 0

    lax.fori_loop(0, NB, step, 0)


def subgrid_kernel(n_vert, per_dev, cap, me_ref, info_ref, image_ref, beam_ref, left_ref, right_ref,
                   out_ref, aterm_ref, where_ref, count_ref, heads_ref):
    me = me_ref[0]
    n = info_ref.shape[0]
    row, col = me // n_vert, me % n_vert

    def zero(i, _):
        count_ref[i] = 0
        return 0

    lax.fori_loop(0, n, zero, 0)
    for i in range(9):
        heads_ref[i] = 0
    live = info_ref[me, 5 * NB]

    def find(station):
        keeper = station // per_dev
        order = count_ref[keeper]
        count_ref[keeper] = order + 1
        return lax.rem(me - keeper + n, n) * cap + order

    def place(b):
        first = find(info_ref[me, 3 * NB + b])
        second = find(info_ref[me, 4 * NB + b])
        owner = info_ref[me, b]
        head = (owner // n_vert - row + 1) * 3 + (owner % n_vert - col + 1)
        head = jnp.where(b < live, head, 4)
        order = heads_ref[head]
        heads_ref[head] = order + 1
        slot = jnp.where(head == 4, NR * CAP + b, jnp.where(head < 4, head, head - 1) * CAP + order)
        where_ref[b] = slot
        return first, second, slot

    def step(i, _):
        places = [place(i * 4 + j) for j in range(4)]
        blocks = []
        for j in range(4):
            p = beam_ref[places[j][0]].astype(F32)
            q = beam_ref[places[j][1]].astype(F32)
            aterm = times(p, q, True)
            aterm_ref[i * 4 + j] = aterm
            blocks.append(times(image_ref[i * 4 + j], aterm, False))
        blocks = dft2(blocks, left_ref[...], right_ref[...], False)
        for j in range(4):
            out_ref[places[j][2]] = blocks[j]
        return 0

    lax.fori_loop(0, NB // 4, step, 0)


def incoming(n_vert, n_au, me, info_ref, visit):
    row, col = me // n_vert, me % n_vert
    for route, (dr, dc) in enumerate(ROUTES):
        sr, sc = row - dr, col - dc
        inside = (sr >= 0) & (sr < n_au) & (sc >= 0) & (sc < n_vert)

        @pl.when(inside)
        def _(route=route, src=sr * n_vert + sc):
            live = info_ref[src, 5 * NB]

            def look(b, count):
                hit = info_ref[src, b] == me

                @pl.when(hit)
                def _():
                    visit(route * CAP + count, info_ref[src, NB + b], info_ref[src, 2 * NB + b])

                return count + hit.astype(jnp.int32)

            lax.fori_loop(0, live, look, jnp.int32(0))

    def own(b, _):
        @pl.when(info_ref[me, b] == me)
        def _():
            visit(NR * CAP + b, info_ref[me, NB + b], info_ref[me, 2 * NB + b])

        return 0

    lax.fori_loop(0, info_ref[me, 5 * NB], own, 0)


def tile_kernel(n_vert, n_au, me_ref, info_ref, got_ref, mine_ref, out_ref, meta_ref, pad_ref):
    def clear(i, _):
        meta_ref[i] = 0
        return 0

    lax.fori_loop(0, 3 * NSLOT, clear, 0)

    def note(slot, row_at, col_at):
        meta_ref[slot] = row_at
        meta_ref[NSLOT + slot] = col_at
        meta_ref[2 * NSLOT + slot] = 1

    incoming(n_vert, n_au, me_ref[0], info_ref, note)
    pad_ref[...] = jnp.zeros_like(pad_ref)
    low = low_half((S, 2 * S))
    blank = jnp.zeros((S, 2 * S), F32)
    blank_rows = jnp.zeros((8, 256), F32)

    def add_all(ref, base, count):
        def step(i, _):
            for j in range(2):
                slot = base + i * 2 + j
                row_at, col_at = meta_ref[slot], meta_ref[NSLOT + slot]
                x = jnp.where(meta_ref[2 * NSLOT + slot] > 0, ref[slot], 0.0)
                top = pl.multiple_of(row_at // 8 * 8, 8)
                start = pl.multiple_of(col_at // 128 * 128, 128)
                for plane in range(2):
                    part = x if plane == 0 else pltpu.roll(x, S, 1)
                    wide = jnp.concatenate([jnp.where(low, part, 0.0), blank], 1)
                    wide = jnp.concatenate([pltpu.roll(wide, col_at % 128, 1), blank_rows], 0)
                    at = (plane, pl.ds(top, S + 8), pl.ds(start, 256))
                    pad_ref[at] += pltpu.roll(wide, row_at % 8, 0)
            return 0

        lax.fori_loop(0, count // 2, step, 0)

    add_all(got_ref, 0, NR * CAP)
    add_all(mine_ref, NR * CAP, NB)
    out_ref[...] = pad_ref[:, :TS, :TS]


def window_kernel(meta_ref, tile_ref, other_ref, taper_ref, model_ref, win_ref, pad_ref):
    total = tile_ref[...]
    for k in range(other_ref.shape[0]):
        total = total + other_ref[k]
    model = total * taper_ref[...][None]
    model_ref[...] = model
    pad_ref[:, :TS, :TS] = model
    pad_ref[:, :TS, TS:] = jnp.zeros((2, TS, 128), F32)
    pad_ref[:, TS:, :] = jnp.zeros((2, 8, TS + 128), F32)
    low = low_half((S, 2 * S))

    def cut(slot):
        row_at, col_at = meta_ref[slot], meta_ref[NSLOT + slot]
        top = pl.multiple_of(row_at // 8 * 8, 8)
        lift = lax.rem(S + 8 - row_at % 8, S + 8)
        start = pl.multiple_of(col_at // 128 * 128, 128)
        shift = lax.rem(256 - col_at % 128, 256)
        parts = []
        for plane in range(2):
            wide = pad_ref[plane, pl.ds(top, S + 8), pl.ds(start, 256)]
            wide = pltpu.roll(wide, shift, 1)[:, : 2 * S]
            parts.append(pltpu.roll(wide, lift, 0)[:S])
        return jnp.where(low, parts[0], pltpu.roll(parts[1], S, 1))

    def step(i, _):
        found = [cut(i * 2 + j) for j in range(2)]
        for j in range(2):
            win_ref[i * 2 + j] = found[j]
        return 0

    lax.fori_loop(0, NSLOT // 2, step, 0)


def degrid_kernel(me_ref, info_ref, where_ref, got_ref, mine_ref, aterm_ref, wave_ref, trig_ref, left_ref,
                  right_ref, out_ref, win_ref):
    rows = trig_ref.shape[2]
    live = info_ref[me_ref[0], 5 * NB]

    def fetch(b, _):
        slot = where_ref[b]

        @pl.when(slot < NR * CAP)
        def _():
            win_ref[b] = got_ref[jnp.minimum(slot, NR * CAP - 1)]

        @pl.when(slot >= NR * CAP)
        def _():
            win_ref[b] = mine_ref[slot]

        return 0

    lax.fori_loop(0, NB, fetch, 0)

    def transform(i, _):
        blocks = [win_ref[i * 4 + j] for j in range(4)]
        blocks = dft2(blocks, left_ref[...], right_ref[...], True)
        for j in range(4):
            win_ref[i * 4 + j] = times(blocks[j], aterm_ref[i * 4 + j], True)
        return 0

    lax.fori_loop(0, NB // 4, transform, 0)

    def predict(b):
        back = win_ref[b]
        hi = back.astype(BF).astype(F32)
        both = jnp.concatenate([hi, back - hi], 0).T.astype(BF)
        ehi, elo = wave_ref[b, :S], wave_ref[b, S:]
        cv, sv = trig_ref[b, :S], trig_ref[b, S:]
        m = jnp.dot(
            jnp.concatenate([both, both], 1),
            jnp.concatenate([ehi, ehi, elo, elo], 0),
            preferred_element_type=F32,
        )
        a_real = m[:S, :rows] + m[S:, rows:]
        a_imag = m[S:, :rows] - m[:S, rows:]
        real = jnp.sum(a_real * cv + a_imag * sv, axis=0, keepdims=True)
        imag = jnp.sum(a_imag * cv - a_real * sv, axis=0, keepdims=True)
        return jnp.concatenate([real, imag], 1) * (1.0 / S)

    def step(i, _):
        found = [predict(i * 2 + j) for j in range(2)]
        for j in range(2):
            out_ref[pl.ds(i * 2 + j, 1), :] = jnp.where(i * 2 + j < live, found[j], 0.0)
        return 0

    lax.fori_loop(0, NB // 2, step, 0)


def info_kernel(n_vert, in_ref, out_ref, send_sem, recv_sem, own_sem):
    n = out_ref.shape[0]
    me = lax.axis_index("au") * n_vert + lax.axis_index("vert")
    barrier = pltpu.get_barrier_semaphore()

    def peer(k):
        t = lax.rem(me + k, n)
        return {"au": t // n_vert, "vert": t % n_vert}

    for k in range(1, n):
        pl.semaphore_signal(barrier, inc=1, device_id=peer(k), device_id_type=MESH)
    own = pltpu.make_async_copy(in_ref, out_ref.at[me], own_sem)
    own.start()
    pl.semaphore_wait(barrier, n - 1)
    copies = []
    for k in range(1, n):
        copies.append(pltpu.make_async_remote_copy(
            in_ref, out_ref.at[me], send_sem.at[k], recv_sem.at[k],
            device_id=peer(k), device_id_type=MESH))
        copies[-1].start()
    own.wait()
    for copy in copies:
        copy.wait()


def beam_exchange_kernel(n_vert, cap, ids_ref, beam_ref, vis_ref, coord_ref, out_ref, image_ref,
                         wave_ref, trig_ref, send_ref, send_sem, recv_sem, own_sem):
    n = out_ref.shape[0]
    me = lax.axis_index("au") * n_vert + lax.axis_index("vert")
    barrier = pltpu.get_barrier_semaphore()

    def peer(k):
        t = lax.rem(me + k, n)
        return {"au": t // n_vert, "vert": t % n_vert}

    for k in range(1, n):
        pl.semaphore_signal(barrier, inc=1, device_id=peer(k), device_id_type=MESH)

    def fill(k, _):
        for j in range(cap):
            send_ref[k, j * S : (j + 1) * S, :] = beam_ref[ids_ref[k * cap + j]]
        return 0

    lax.fori_loop(0, n, fill, 0)
    own = pltpu.make_async_copy(send_ref.at[0], out_ref.at[0], own_sem)
    own.start()
    pl.semaphore_wait(barrier, n - 1)
    copies = []
    for k in range(1, n):
        copies.append(pltpu.make_async_remote_copy(
            send_ref.at[k], out_ref.at[k], send_sem.at[k], recv_sem.at[k],
            device_id=peer(k), device_id_type=MESH))
        copies[-1].start()
    make_images(vis_ref, coord_ref, image_ref, wave_ref, trig_ref)
    own.wait()
    for copy in copies:
        copy.wait()


def route_kernel(n_au, n_vert, sign, in_ref, out_ref, send_sem, recv_sem):
    row, col = lax.axis_index("au"), lax.axis_index("vert")
    barrier = pltpu.get_barrier_semaphore()

    def inside(dr, dc):
        return (row + dr >= 0) & (row + dr < n_au) & (col + dc >= 0) & (col + dc < n_vert)

    for dr, dc in ROUTES:
        @pl.when(inside(dr, dc))
        def _():
            pl.semaphore_signal(barrier, inc=1, device_id={"au": row + dr, "vert": col + dc},
                                device_id_type=MESH)
    tall = 1 + jnp.minimum(row, 1) + jnp.minimum(n_au - 1 - row, 1)
    wide = 1 + jnp.minimum(col, 1) + jnp.minimum(n_vert - 1 - col, 1)
    pl.semaphore_wait(barrier, tall * wide - 1)

    def copy_of(i, dr, dc):
        at = pl.ds(i * CAP, CAP)
        return pltpu.make_async_remote_copy(
            in_ref.at[at], out_ref.at[at], send_sem.at[i], recv_sem.at[i],
            device_id={"au": row + dr, "vert": col + dc}, device_id_type=MESH)

    for i, (dr, dc) in enumerate(ROUTES):
        dr, dc = sign * dr, sign * dc

        @pl.when(inside(dr, dc))
        def _():
            copy_of(i, dr, dc).start()
    for i, (dr, dc) in enumerate(ROUTES):
        dr, dc = sign * dr, sign * dc

        @pl.when(inside(dr, dc))
        def _():
            copy_of(i, dr, dc).wait_send()

        @pl.when(inside(-dr, -dc))
        def _():
            copy_of(i, dr, dc).wait_recv()


def tile_exchange_kernel(in_ref, out_ref, send_sem, recv_sem):
    n = out_ref.shape[0] + 1
    me = lax.axis_index("af")
    barrier = pltpu.get_barrier_semaphore()
    for k in range(1, n):
        pl.semaphore_signal(barrier, inc=1, device_id={"af": lax.rem(me + k, n)}, device_id_type=MESH)
    pl.semaphore_wait(barrier, n - 1)
    copies = []
    for k in range(1, n):
        copies.append(pltpu.make_async_remote_copy(
            in_ref, out_ref.at[k - 1], send_sem.at[k - 1], recv_sem.at[k - 1],
            device_id={"af": lax.rem(me + k, n)}, device_id_type=MESH))
        copies[-1].start()
    for copy in copies:
        copy.wait()


SMEM = pl.BlockSpec(memory_space=pltpu.SMEM)
VMEM = pl.BlockSpec(memory_space=pltpu.VMEM)
ANY = pl.BlockSpec(memory_space=pl.ANY)


def shape(*dims, dtype=F32):
    return jax.ShapeDtypeStruct(dims, dtype)


def local_call(kernel, in_specs, out_specs, out_shape, scratch=()):
    return pl.pallas_call(
        kernel, in_specs=in_specs, out_specs=out_specs, out_shape=out_shape,
        scratch_shapes=list(scratch),
        compiler_params=pltpu.CompilerParams(vmem_limit_bytes=VMEM_LIMIT))


def remote_call(kernel, ident, in_specs, out_shape, scratch, out_specs=ANY):
    return pl.pallas_call(
        kernel, in_specs=in_specs, out_specs=out_specs, out_shape=out_shape, scratch_shapes=scratch,
        compiler_params=pltpu.CompilerParams(
            collective_id=ident, has_side_effects=True, vmem_limit_bytes=VMEM_LIMIT))


def body(visib, coords, owner, offsets, stations, live, beams, taper):
    n_au, n_vert, n_af = lax.axis_size("au"), lax.axis_size("vert"), lax.axis_size("af")
    n = n_au * n_vert
    per_dev = beams.shape[1]
    cap = 2 * NB // n + 2
    me = lax.axis_index("au") * n_vert + lax.axis_index("vert")
    mine = me.astype(jnp.int32).reshape(1)
    signal, places = visib[0], coords[0]
    rows2 = signal.shape[1]
    info = jnp.concatenate(
        [owner[0], offsets[0, :, 0], offsets[0, :, 1], stations[0, :, 0], stations[0, :, 1],
         jnp.broadcast_to(live[0, 0], (128 - 5 * NB,))])
    info = remote_call(
        lambda *refs: info_kernel(n_vert, *refs), 5, [VMEM], shape(n, 1, 128, dtype=jnp.int32),
        [pltpu.SemaphoreType.DMA((n,)), pltpu.SemaphoreType.DMA((n,)), pltpu.SemaphoreType.DMA],
        out_specs=VMEM,
    )(info.reshape(1, 128)).reshape(n, 128)
    left, right, right_conj = constants()

    asked = jnp.roll(info[:, 3 * NB : 5 * NB], -me, axis=0).reshape(n, 2, NB)
    asked = asked.transpose(0, 2, 1).reshape(n, 2 * NB)
    hit = asked // per_dev == me
    entry = jnp.arange(2 * NB, dtype=jnp.int32)
    order = jnp.sum((hit[:, None, :] & (entry[None, :] < entry[:, None])[None]).astype(jnp.int32), axis=2)
    pick = hit[:, None, :] & (order[:, None, :] == jnp.arange(cap, dtype=jnp.int32)[None, :, None])
    ids = jnp.sum(jnp.where(pick, (asked % per_dev)[:, None, :], 0), axis=2).reshape(n * cap)
    found, images, waves, trigs = remote_call(
        lambda *refs: beam_exchange_kernel(n_vert, cap, *refs), 1, [SMEM] + [VMEM] * 3,
        [shape(n, cap * S, 2 * S, dtype=BF), shape(NB, S, 2 * S),
         shape(NB, 2 * S, rows2, dtype=BF), shape(NB, 2 * S, rows2 // 2)],
        [pltpu.VMEM((n, cap * S, 2 * S), BF), pltpu.SemaphoreType.DMA((n,)),
         pltpu.SemaphoreType.DMA((n,)), pltpu.SemaphoreType.DMA],
        out_specs=[ANY, VMEM, VMEM, VMEM],
    )(ids, beams[0].reshape(per_dev, S, 2 * S), signal, places)

    subgrids, aterms, slots = local_call(
        lambda *refs: subgrid_kernel(n_vert, per_dev, cap, *refs),
        [SMEM, SMEM] + [VMEM] * 4, [VMEM, VMEM, SMEM],
        [shape(NSLOT, S, 2 * S), shape(NB, S, 2 * S), shape(NB, dtype=jnp.int32)],
        [pltpu.SMEM((n,), jnp.int32), pltpu.SMEM((9,), jnp.int32)],
    )(mine, info, images, found.reshape(n * cap, S, 2 * S), left, right)

    def routed(values, sign, ident):
        return remote_call(
            lambda *refs: route_kernel(n_au, n_vert, sign, *refs), ident, [ANY],
            shape(NR * CAP, S, 2 * S),
            [pltpu.SemaphoreType.DMA((NR,)), pltpu.SemaphoreType.DMA((NR,))])(values)

    arrived = routed(subgrids, 1, 2)
    tile, meta = local_call(
        lambda *refs: tile_kernel(n_vert, n_au, *refs), [SMEM, SMEM, VMEM, VMEM], [VMEM, SMEM],
        [shape(2, TS, TS), shape(3 * NSLOT, dtype=jnp.int32)],
        [pltpu.VMEM((2, TS + 8, TS + 128), F32)])(mine, info, arrived, subgrids)
    others = remote_call(
        tile_exchange_kernel, 3, [ANY], shape(n_af - 1, 2, TS, TS),
        [pltpu.SemaphoreType.DMA((n_af - 1,)), pltpu.SemaphoreType.DMA((n_af - 1,))])(tile)
    model_grid, windows = local_call(
        window_kernel, [SMEM] + [VMEM] * 3, [VMEM, VMEM],
        [shape(2, TS, TS), shape(NSLOT, S, 2 * S)], [pltpu.VMEM((2, TS + 8, TS + 128), F32)],
    )(meta, tile, others, taper)
    returned = routed(windows, -1, 4)
    result = local_call(
        degrid_kernel, [SMEM] * 3 + [VMEM] * 7, VMEM, shape(NB, rows2), [pltpu.VMEM((NB, S, 2 * S), F32)],
    )(mine, info, slots, returned, windows, aterms, waves, trigs, left, right_conj)
    return (result[None], model_grid)


def solution(mesh):
    placed = (
        P("af", ("au", "vert"), None),
        P("af", ("au", "vert"), None),
        P("af", ("au", "vert")),
        P("af", ("au", "vert"), None),
        P("af", ("au", "vert"), None),
        P("af", ("au", "vert")),
        P("af", ("au", "vert"), None),
        P("au", "vert"),
    )
    return jax.shard_map(
        body,
        mesh=mesh,
        in_specs=placed,
        out_specs=(P("af", ("au", "vert"), None), P(None, "au", "vert")),
        check_vma=False,
    )
```

```python
import math

import jax
import jax.numpy as jnp
import numpy as np
from jax import lax
from jax.experimental import pallas as pl
from jax.experimental.pallas import tpu as pltpu
from jax.sharding import PartitionSpec as P

S = 64
CAP = 2
NB = 16
TS = 512
BF = jnp.bfloat16
F32 = jnp.float32
MESH = pl.DeviceIdType.MESH
ROUTES = tuple((r, c) for r in (-1, 0, 1) for c in (-1, 0, 1) if (r, c) != (0, 0))
NR = len(ROUTES)
NSLOT = NR * CAP + NB
VMEM_LIMIT = 32 * 1024 * 1024


def fit(fn, count):
    k = np.arange(400)
    z = 0.125 * (1.0 + np.cos(np.pi * (k + 0.5) / 400))
    cheb = np.polynomial.chebyshev.Chebyshev.fit(z, fn(np.sqrt(z)), count - 1, domain=[0, 0.25])
    return [float(v) for v in cheb.convert(kind=np.polynomial.Polynomial).coef]


COS = fit(lambda t: np.cos(2 * np.pi * t), 8)
SIN = fit(lambda t: np.sin(2 * np.pi * t) / t, 8)


def dft_tables():
    pos = np.arange(S)
    ang = (pos[:, None] * pos[None, :] % S) * (2.0 * np.pi / S)
    return np.cos(ang) / math.sqrt(S), -np.sin(ang) / math.sqrt(S)


def split_np(x):
    x = x.astype(np.float32)
    hi = x.astype(BF).astype(np.float32)
    return hi, (x - hi).astype(BF).astype(np.float32)


def constants():
    fr, fi = dft_tables()
    hi, lo = split_np(np.concatenate([fr, fi], 0))
    left = np.concatenate([hi, hi, lo, lo], 1)
    out = [left]
    for sign in (1, -1):
        right = np.concatenate(
            [np.concatenate([fr, sign * fi], 1), np.concatenate([-sign * fi, fr], 1)], 0
        )
        hi, lo = split_np(right)
        out.append(np.concatenate([np.concatenate([hi, hi], 0), np.concatenate([lo, lo], 0)], 1))
    return [v.astype(BF) for v in out]


def split(x):
    hi = x.astype(BF)
    return hi, (x - hi.astype(F32)).astype(BF)


def horner(coefs, z):
    acc = jnp.full(z.shape, coefs[-1], F32)
    for c in coefs[-2::-1]:
        acc = acc * z + c
    return acc


def cos_sin(turns):
    t = turns - jnp.round(turns)
    z = t * t
    return horner(COS, z), horner(SIN, z) * t


def phases(u):
    j = lax.broadcasted_iota(jnp.int32, (8, u.shape[1]), 0).astype(F32)
    c1, s1 = cos_sin(u * (j * (1.0 / 64)))
    c2, s2 = cos_sin(u * (j * 0.125 - 0.5))
    cs, ss = [], []
    for k in range(8):
        ck, sk = c2[k : k + 1], s2[k : k + 1]
        cs.append(ck * c1 - sk * s1)
        ss.append(sk * c1 + ck * s1)
    return jnp.concatenate(cs, 0), jnp.concatenate(ss, 0)


def low_half(shape):
    return lax.broadcasted_iota(jnp.int32, shape, 1) < S


def rotate(x):
    y = pltpu.roll(x, S, 1)
    return jnp.where(low_half(x.shape), -y, y)


def times(x, a, conj):
    low = low_half(x.shape)
    ra = pltpu.roll(a, S, 1)
    rr = jnp.where(low, a, ra)
    ii = jnp.where(low, ra, a)
    y = pltpu.roll(x, S, 1) * ii
    sgn = low if conj else jnp.logical_not(low)
    return x * rr + jnp.where(sgn, y, -y)


def dft2(blocks, left, right, conj):
    width = 2 * S
    hi, lo = split(jnp.concatenate(blocks, 1) if len(blocks) > 1 else blocks[0])
    m = jnp.dot(left, jnp.concatenate([hi, lo, hi, lo], 0), preferred_element_type=F32)
    rows = []
    for i in range(len(blocks)):
        part = m[:, i * width : (i + 1) * width]
        turned = rotate(part[S:])
        rows.append(part[:S] - turned if conj else part[:S] + turned)
    hi, lo = split(jnp.concatenate(rows, 0))
    m = jnp.dot(jnp.concatenate([hi, lo], 1), right, preferred_element_type=F32)
    m = m[:, :width] + m[:, width:]
    return [m[i * S : (i + 1) * S] for i in range(len(blocks))]


def make_images(vis_ref, coord_ref, out_ref, wave_ref, trig_ref):
    rows = vis_ref.shape[1] // 2

    def step(b, _):
        at = pl.ds(b, 1)
        cu, su = phases(coord_ref[at, :rows])
        cv, sv = phases(coord_ref[at, rows:])
        vr, vi = vis_ref[at, :rows], vis_ref[at, rows:]
        trig_ref[b, :S] = cv
        trig_ref[b, S:] = sv
        ahi, alo = split(jnp.concatenate([cu, su], 0))
        wave_ref[b, :S, :rows] = ahi[:S]
        wave_ref[b, :S, rows:] = ahi[S:]
        wave_ref[b, S:, :rows] = alo[:S]
        wave_ref[b, S:, rows:] = alo[S:]
        bhi, blo = split(jnp.concatenate([vr * cv - vi * sv, vr * sv + vi * cv], 0))
        m = lax.dot_general(
            jnp.concatenate([ahi, alo], 0),
            jnp.concatenate([bhi, blo], 0),
            (((1,), (1,)), ((), ())),
            preferred_element_type=F32,
        )
        m = m[: 2 * S] + m[2 * S :]
        m = m[:, : 2 * S] + m[:, 2 * S :]
        out_ref[b] = (m[:S] + rotate(m[S:])) * (1.0 / math.sqrt(rows))
        return 0

    lax.fori_loop(0, NB, step, 0)


def subgrid_kernel(n_vert, per_dev, cap, me_ref, info_ref, image_ref, beam_ref, left_ref, right_ref,
                   out_ref, aterm_ref, where_ref, count_ref, heads_ref):
    me = me_ref[0]
    n = info_ref.shape[0]
    row, col = me // n_vert, me % n_vert

    def zero(i, _):
        count_ref[i] = 0
        return 0

    lax.fori_loop(0, n, zero, 0)
    for i in range(9):
        heads_ref[i] = 0
    live = info_ref[me, 5 * NB]

    def find(station):
        keeper = station // per_dev
        order = count_ref[keeper]
        count_ref[keeper] = order + 1
        return lax.rem(me - keeper + n, n) * cap + order

    def place(b):
        first = find(info_ref[me, 3 * NB + b])
        second = find(info_ref[me, 4 * NB + b])
        owner = info_ref[me, b]
        head = (owner // n_vert - row + 1) * 3 + (owner % n_vert - col + 1)
        head = jnp.where(b < live, head, 4)
        order = heads_ref[head]
        heads_ref[head] = order + 1
        slot = jnp.where(head == 4, NR * CAP + b, jnp.where(head < 4, head, head - 1) * CAP + order)
        where_ref[b] = slot
        return first, second, slot

    def step(i, _):
        places = [place(i * 4 + j) for j in range(4)]
        blocks = []
        for j in range(4):
            p = beam_ref[places[j][0]].astype(F32)
            q = beam_ref[places[j][1]].astype(F32)
            aterm = times(p, q, True)
            aterm_ref[i * 4 + j] = aterm
            blocks.append(times(image_ref[i * 4 + j], aterm, False))
        blocks = dft2(blocks, left_ref[...], right_ref[...], False)
        for j in range(4):
            out_ref[places[j][2]] = blocks[j]
        return 0

    lax.fori_loop(0, NB // 4, step, 0)


def incoming(n_vert, n_au, me, info_ref, visit):
    row, col = me // n_vert, me % n_vert
    for route, (dr, dc) in enumerate(ROUTES):
        sr, sc = row - dr, col - dc
        inside = (sr >= 0) & (sr < n_au) & (sc >= 0) & (sc < n_vert)

        @pl.when(inside)
        def _(route=route, src=sr * n_vert + sc):
            live = info_ref[src, 5 * NB]

            def look(b, count):
                hit = info_ref[src, b] == me

                @pl.when(hit)
                def _():
                    visit(route * CAP + count, info_ref[src, NB + b], info_ref[src, 2 * NB + b])

                return count + hit.astype(jnp.int32)

            lax.fori_loop(0, live, look, jnp.int32(0))

    def own(b, _):
        @pl.when(info_ref[me, b] == me)
        def _():
            visit(NR * CAP + b, info_ref[me, NB + b], info_ref[me, 2 * NB + b])

        return 0

    lax.fori_loop(0, info_ref[me, 5 * NB], own, 0)


def tile_kernel(n_vert, n_au, me_ref, info_ref, got_ref, mine_ref, out_ref, meta_ref, pad_ref):
    def clear(i, _):
        meta_ref[i] = 0
        return 0

    lax.fori_loop(0, 3 * NSLOT, clear, 0)

    def note(slot, row_at, col_at):
        meta_ref[slot] = row_at
        meta_ref[NSLOT + slot] = col_at
        meta_ref[2 * NSLOT + slot] = 1

    incoming(n_vert, n_au, me_ref[0], info_ref, note)
    pad_ref[...] = jnp.zeros_like(pad_ref)
    low = low_half((S, 2 * S))
    blank = jnp.zeros((S, 2 * S), F32)
    blank_rows = jnp.zeros((8, 256), F32)

    def add_all(ref, base, count):
        def step(i, _):
            for j in range(2):
                slot = base + i * 2 + j
                row_at, col_at = meta_ref[slot], meta_ref[NSLOT + slot]
                x = jnp.where(meta_ref[2 * NSLOT + slot] > 0, ref[slot], 0.0)
                top = pl.multiple_of(row_at // 8 * 8, 8)
                start = pl.multiple_of(col_at // 128 * 128, 128)
                for plane in range(2):
                    part = x if plane == 0 else pltpu.roll(x, S, 1)
                    wide = jnp.concatenate([jnp.where(low, part, 0.0), blank], 1)
                    wide = jnp.concatenate([pltpu.roll(wide, col_at % 128, 1), blank_rows], 0)
                    at = (plane, pl.ds(top, S + 8), pl.ds(start, 256))
                    pad_ref[at] += pltpu.roll(wide, row_at % 8, 0)
            return 0

        lax.fori_loop(0, count // 2, step, 0)

    add_all(got_ref, 0, NR * CAP)
    add_all(mine_ref, NR * CAP, NB)
    out_ref[...] = pad_ref[:, :TS, :TS]


def window_kernel(meta_ref, tile_ref, other_ref, taper_ref, model_ref, win_ref, pad_ref):
    total = tile_ref[...]
    for k in range(other_ref.shape[0]):
        total = total + other_ref[k]
    model = total * taper_ref[...][None]
    model_ref[...] = model
    pad_ref[:, :TS, :TS] = model
    pad_ref[:, :TS, TS:] = jnp.zeros((2, TS, 128), F32)
    pad_ref[:, TS:, :] = jnp.zeros((2, 8, TS + 128), F32)
    low = low_half((S, 2 * S))

    def cut(slot):
        row_at, col_at = meta_ref[slot], meta_ref[NSLOT + slot]
        top = pl.multiple_of(row_at // 8 * 8, 8)
        lift = lax.rem(S + 8 - row_at % 8, S + 8)
        start = pl.multiple_of(col_at // 128 * 128, 128)
        shift = lax.rem(256 - col_at % 128, 256)
        parts = []
        for plane in range(2):
            wide = pad_ref[plane, pl.ds(top, S + 8), pl.ds(start, 256)]
            wide = pltpu.roll(wide, shift, 1)[:, : 2 * S]
            parts.append(pltpu.roll(wide, lift, 0)[:S])
        return jnp.where(low, parts[0], pltpu.roll(parts[1], S, 1))

    def step(i, _):
        found = [cut(i * 2 + j) for j in range(2)]
        for j in range(2):
            win_ref[i * 2 + j] = found[j]
        return 0

    lax.fori_loop(0, NSLOT // 2, step, 0)


def degrid_kernel(me_ref, info_ref, where_ref, got_ref, mine_ref, aterm_ref, wave_ref, trig_ref, left_ref,
                  right_ref, out_ref, win_ref):
    rows = trig_ref.shape[2]
    live = info_ref[me_ref[0], 5 * NB]

    def fetch(b, _):
        slot = where_ref[b]

        @pl.when(slot < NR * CAP)
        def _():
            win_ref[b] = got_ref[jnp.minimum(slot, NR * CAP - 1)]

        @pl.when(slot >= NR * CAP)
        def _():
            win_ref[b] = mine_ref[slot]

        return 0

    lax.fori_loop(0, NB, fetch, 0)

    def transform(i, _):
        blocks = [win_ref[i * 4 + j] for j in range(4)]
        blocks = dft2(blocks, left_ref[...], right_ref[...], True)
        for j in range(4):
            win_ref[i * 4 + j] = times(blocks[j], aterm_ref[i * 4 + j], True)
        return 0

    lax.fori_loop(0, NB // 4, transform, 0)

    def predict(b):
        back = win_ref[b]
        hi = back.astype(BF).astype(F32)
        both = jnp.concatenate([hi, back - hi], 0).T.astype(BF)
        ehi, elo = wave_ref[b, :S], wave_ref[b, S:]
        cv, sv = trig_ref[b, :S], trig_ref[b, S:]
        m = jnp.dot(
            jnp.concatenate([both, both], 1),
            jnp.concatenate([ehi, ehi, elo, elo], 0),
            preferred_element_type=F32,
        )
        a_real = m[:S, :rows] + m[S:, rows:]
        a_imag = m[S:, :rows] - m[:S, rows:]
        real = jnp.sum(a_real * cv + a_imag * sv, axis=0, keepdims=True)
        imag = jnp.sum(a_imag * cv - a_real * sv, axis=0, keepdims=True)
        return jnp.concatenate([real, imag], 1) * (1.0 / S)

    def step(i, _):
        found = [predict(i * 2 + j) for j in range(2)]
        for j in range(2):
            out_ref[pl.ds(i * 2 + j, 1), :] = jnp.where(i * 2 + j < live, found[j], 0.0)
        return 0

    lax.fori_loop(0, NB // 2, step, 0)


def info_kernel(n_vert, in_ref, out_ref, send_sem, recv_sem, own_sem):
    n = out_ref.shape[0]
    me = lax.axis_index("au") * n_vert + lax.axis_index("vert")
    barrier = pltpu.get_barrier_semaphore()

    def peer(k):
        t = lax.rem(me + k, n)
        return {"au": t // n_vert, "vert": t % n_vert}

    for k in range(1, n):
        pl.semaphore_signal(barrier, inc=1, device_id=peer(k), device_id_type=MESH)
    own = pltpu.make_async_copy(in_ref, out_ref.at[me], own_sem)
    own.start()
    pl.semaphore_wait(barrier, n - 1)
    copies = []
    for k in range(1, n):
        copies.append(pltpu.make_async_remote_copy(
            in_ref, out_ref.at[me], send_sem.at[k], recv_sem.at[k],
            device_id=peer(k), device_id_type=MESH))
        copies[-1].start()
    own.wait()
    for copy in copies:
        copy.wait()


def beam_exchange_kernel(n_vert, cap, ids_ref, beam_ref, vis_ref, coord_ref, out_ref, image_ref,
                         wave_ref, trig_ref, send_ref, send_sem, recv_sem, own_sem):
    n = out_ref.shape[0]
    me = lax.axis_index("au") * n_vert + lax.axis_index("vert")
    barrier = pltpu.get_barrier_semaphore()

    def peer(k):
        t = lax.rem(me + k, n)
        return {"au": t // n_vert, "vert": t % n_vert}

    for k in range(1, n):
        pl.semaphore_signal(barrier, inc=1, device_id=peer(k), device_id_type=MESH)

    def fill(k, _):
        for j in range(cap):
            send_ref[k, j * S : (j + 1) * S, :] = beam_ref[ids_ref[k * cap + j]]
        return 0

    lax.fori_loop(0, n, fill, 0)
    own = pltpu.make_async_copy(send_ref.at[0], out_ref.at[0], own_sem)
    own.start()
    pl.semaphore_wait(barrier, n - 1)
    copies = []
    for k in sorted(range(1, n), key=lambda k: -min(k % n_vert, -k % n_vert)):
        copies.append(pltpu.make_async_remote_copy(
            send_ref.at[k], out_ref.at[k], send_sem.at[k], recv_sem.at[k],
            device_id=peer(k), device_id_type=MESH))
        copies[-1].start()
    make_images(vis_ref, coord_ref, image_ref, wave_ref, trig_ref)
    own.wait()
    for copy in copies:
        copy.wait()


def route_kernel(n_au, n_vert, sign, in_ref, out_ref, send_sem, recv_sem):
    row, col = lax.axis_index("au"), lax.axis_index("vert")
    barrier = pltpu.get_barrier_semaphore()

    def inside(dr, dc):
        return (row + dr >= 0) & (row + dr < n_au) & (col + dc >= 0) & (col + dc < n_vert)

    for dr, dc in ROUTES:
        @pl.when(inside(dr, dc))
        def _():
            pl.semaphore_signal(barrier, inc=1, device_id={"au": row + dr, "vert": col + dc},
                                device_id_type=MESH)
    tall = 1 + jnp.minimum(row, 1) + jnp.minimum(n_au - 1 - row, 1)
    wide = 1 + jnp.minimum(col, 1) + jnp.minimum(n_vert - 1 - col, 1)
    pl.semaphore_wait(barrier, tall * wide - 1)

    def copy_of(i, dr, dc):
        at = pl.ds(i * CAP, CAP)
        return pltpu.make_async_remote_copy(
            in_ref.at[at], out_ref.at[at], send_sem.at[i], recv_sem.at[i],
            device_id={"au": row + dr, "vert": col + dc}, device_id_type=MESH)

    for i, (dr, dc) in enumerate(ROUTES):
        dr, dc = sign * dr, sign * dc

        @pl.when(inside(dr, dc))
        def _():
            copy_of(i, dr, dc).start()
    for i, (dr, dc) in enumerate(ROUTES):
        dr, dc = sign * dr, sign * dc

        @pl.when(inside(dr, dc))
        def _():
            copy_of(i, dr, dc).wait_send()

        @pl.when(inside(-dr, -dc))
        def _():
            copy_of(i, dr, dc).wait_recv()


def tile_exchange_kernel(in_ref, out_ref, send_sem, recv_sem):
    n = out_ref.shape[0] + 1
    me = lax.axis_index("af")
    barrier = pltpu.get_barrier_semaphore()
    for k in range(1, n):
        pl.semaphore_signal(barrier, inc=1, device_id={"af": lax.rem(me + k, n)}, device_id_type=MESH)
    pl.semaphore_wait(barrier, n - 1)
    copies = []
    for k in range(1, n):
        copies.append(pltpu.make_async_remote_copy(
            in_ref, out_ref.at[k - 1], send_sem.at[k - 1], recv_sem.at[k - 1],
            device_id={"af": lax.rem(me + k, n)}, device_id_type=MESH))
        copies[-1].start()
    for copy in copies:
        copy.wait()


SMEM = pl.BlockSpec(memory_space=pltpu.SMEM)
VMEM = pl.BlockSpec(memory_space=pltpu.VMEM)
ANY = pl.BlockSpec(memory_space=pl.ANY)


def shape(*dims, dtype=F32):
    return jax.ShapeDtypeStruct(dims, dtype)


def local_call(kernel, in_specs, out_specs, out_shape, scratch=()):
    return pl.pallas_call(
        kernel, in_specs=in_specs, out_specs=out_specs, out_shape=out_shape,
        scratch_shapes=list(scratch),
        compiler_params=pltpu.CompilerParams(vmem_limit_bytes=VMEM_LIMIT))


def remote_call(kernel, ident, in_specs, out_shape, scratch, out_specs=ANY):
    return pl.pallas_call(
        kernel, in_specs=in_specs, out_specs=out_specs, out_shape=out_shape, scratch_shapes=scratch,
        compiler_params=pltpu.CompilerParams(
            collective_id=ident, has_side_effects=True, vmem_limit_bytes=VMEM_LIMIT))


def body(visib, coords, owner, offsets, stations, live, beams, taper):
    n_au, n_vert, n_af = lax.axis_size("au"), lax.axis_size("vert"), lax.axis_size("af")
    n = n_au * n_vert
    per_dev = beams.shape[1]
    cap = 2 * NB // n + 2
    me = lax.axis_index("au") * n_vert + lax.axis_index("vert")
    mine = me.astype(jnp.int32).reshape(1)
    signal, places = visib[0], coords[0]
    rows2 = signal.shape[1]
    info = jnp.concatenate(
        [owner[0], offsets[0, :, 0], offsets[0, :, 1], stations[0, :, 0], stations[0, :, 1],
         jnp.broadcast_to(live[0, 0], (128 - 5 * NB,))])
    info = remote_call(
        lambda *refs: info_kernel(n_vert, *refs), 5, [VMEM], shape(n, 1, 128, dtype=jnp.int32),
        [pltpu.SemaphoreType.DMA((n,)), pltpu.SemaphoreType.DMA((n,)), pltpu.SemaphoreType.DMA],
        out_specs=VMEM,
    )(info.reshape(1, 128)).reshape(n, 128)
    left, right, right_conj = constants()

    asked = jnp.roll(info[:, 3 * NB : 5 * NB], -me, axis=0).reshape(n, 2, NB)
    asked = asked.transpose(0, 2, 1).reshape(n, 2 * NB)
    hit = asked // per_dev == me
    entry = jnp.arange(2 * NB, dtype=jnp.int32)
    order = jnp.sum((hit[:, None, :] & (entry[None, :] < entry[:, None])[None]).astype(jnp.int32), axis=2)
    pick = hit[:, None, :] & (order[:, None, :] == jnp.arange(cap, dtype=jnp.int32)[None, :, None])
    ids = jnp.sum(jnp.where(pick, (asked % per_dev)[:, None, :], 0), axis=2).reshape(n * cap)
    found, images, waves, trigs = remote_call(
        lambda *refs: beam_exchange_kernel(n_vert, cap, *refs), 1, [SMEM] + [VMEM] * 3,
        [shape(n, cap * S, 2 * S, dtype=BF), shape(NB, S, 2 * S),
         shape(NB, 2 * S, rows2, dtype=BF), shape(NB, 2 * S, rows2 // 2)],
        [pltpu.VMEM((n, cap * S, 2 * S), BF), pltpu.SemaphoreType.DMA((n,)),
         pltpu.SemaphoreType.DMA((n,)), pltpu.SemaphoreType.DMA],
        out_specs=[ANY, VMEM, VMEM, VMEM],
    )(ids, beams[0].reshape(per_dev, S, 2 * S), signal, places)

    subgrids, aterms, slots = local_call(
        lambda *refs: subgrid_kernel(n_vert, per_dev, cap, *refs),
        [SMEM, SMEM] + [VMEM] * 4, [VMEM, VMEM, SMEM],
        [shape(NSLOT, S, 2 * S), shape(NB, S, 2 * S), shape(NB, dtype=jnp.int32)],
        [pltpu.SMEM((n,), jnp.int32), pltpu.SMEM((9,), jnp.int32)],
    )(mine, info, images, found.reshape(n * cap, S, 2 * S), left, right)

    def routed(values, sign, ident):
        return remote_call(
            lambda *refs: route_kernel(n_au, n_vert, sign, *refs), ident, [ANY],
            shape(NR * CAP, S, 2 * S),
            [pltpu.SemaphoreType.DMA((NR,)), pltpu.SemaphoreType.DMA((NR,))])(values)

    arrived = routed(subgrids, 1, 2)
    tile, meta = local_call(
        lambda *refs: tile_kernel(n_vert, n_au, *refs), [SMEM, SMEM, VMEM, VMEM], [VMEM, SMEM],
        [shape(2, TS, TS), shape(3 * NSLOT, dtype=jnp.int32)],
        [pltpu.VMEM((2, TS + 8, TS + 128), F32)])(mine, info, arrived, subgrids)
    others = remote_call(
        tile_exchange_kernel, 3, [ANY], shape(n_af - 1, 2, TS, TS),
        [pltpu.SemaphoreType.DMA((n_af - 1,)), pltpu.SemaphoreType.DMA((n_af - 1,))])(tile)
    model_grid, windows = local_call(
        window_kernel, [SMEM] + [VMEM] * 3, [VMEM, VMEM],
        [shape(2, TS, TS), shape(NSLOT, S, 2 * S)], [pltpu.VMEM((2, TS + 8, TS + 128), F32)],
    )(meta, tile, others, taper)
    returned = routed(windows, -1, 4)
    result = local_call(
        degrid_kernel, [SMEM] * 3 + [VMEM] * 7, VMEM, shape(NB, rows2), [pltpu.VMEM((NB, S, 2 * S), F32)],
    )(mine, info, slots, returned, windows, aterms, waves, trigs, left, right_conj)
    return (result[None], model_grid)


def solution(mesh):
    placed = (
        P("af", ("au", "vert"), None),
        P("af", ("au", "vert"), None),
        P("af", ("au", "vert")),
        P("af", ("au", "vert"), None),
        P("af", ("au", "vert"), None),
        P("af", ("au", "vert")),
        P("af", ("au", "vert"), None),
        P("au", "vert"),
    )
    return jax.shard_map(
        body,
        mesh=mesh,
        in_specs=placed,
        out_specs=(P("af", ("au", "vert"), None), P(None, "au", "vert")),
        check_vma=False,
    )
```
